512 devices in a mesh: ctx: 32 (over x_lo, y, core), head: 16 (over z, x_hi).
Axes of the slice: x: 4 (x_hi: 2, x_lo: 2; x = x_hi * 2 + x_lo), y: 8, z: 8, core: 2. Of those that a mesh axis runs over, the one named last changes fastest.
Arguments:
- latent_keys: bfloat16 [4096, 576], P('ctx'), may hold values from -6 to 6
- index_keys: bfloat16 [4096, 128], P('ctx'), may hold values from -6 to 6
- main_query: bfloat16 [4096, 73728], P('ctx', 'head'), may hold values from -107 to 107
- index_query: bfloat16 [4096, 8192], P('ctx', 'head'), may hold values from -10 to 10
- index_weight: bfloat16 [4096, 64], P('ctx', 'head'), may hold values from 0.029907227 to 0.29882812
- segment_ids: int32 [4096], replicated, may hold values from 0 to 7, never falling along the last dimension, each value on 1 to 1024 neighbouring positions
- block_order: int32 [64], replicated, may hold values from 0 to 63, each once
Outputs:
- kl: float32 [4096], P('ctx')
The draws below stay inside these ranges and needn't reach their ends.
Inputs may be any that keep to these rules, and one draw needn't show every extreme that they name: `segment_ids`: never falls along the sequence; each document holds 1 to 1024 positions and one holds exactly that many. `block_order`: each block number appears once.
All inputs are finite; a program needn't handle non-finite values.
Results may differ from the reference program's by a relative error of at most 0.0003.
Values may be sent and summed in bfloat16 or wider, within the bound.
A program may use at most 64 MiB of HBM per device.

```python
import math
import jax
import jax.numpy as jnp
import numpy as np
from jax import lax

HEADS = 128
IHEADS = 64
IDIM = 128
KDIM = 576
HALF = 64
SEQ = 4096
N_CTX = 32


def latent_table(key):
    noise = jax.random.normal(jax.random.fold_in(key, 101), (SEQ, KDIM), jnp.float32)
    return jnp.clip(noise, -6.0, 6.0)


def index_table(key):
    noise = jax.random.normal(jax.random.fold_in(key, 202), (SEQ, IDIM), jnp.float32)
    return jnp.clip(noise, -6.0, 6.0)


def drawn_flags(key):
    return jnp.arange(SEQ) % 16 == 0


def draw_latent_keys(key, part):
    return latent_table(key).astype(jnp.bfloat16)


def draw_index_keys(key, part):
    return index_table(key).astype(jnp.bfloat16)


def draw_main_query(key, part):
    noise = jax.random.normal(jax.random.fold_in(key, 404), (SEQ, HEADS, KDIM), jnp.float32)
    values = jnp.clip(noise, -6.0, 6.0)
    target_score = 120.0 + 200.0 * jax.random.uniform(jax.random.fold_in(key, 405), (SEQ, HEADS), jnp.float32)
    factor = target_score * 192.0 ** 0.5 / KDIM
    copied = factor[:, :, None] * latent_table(key)[:, None, :]
    values = jnp.where(drawn_flags(key)[:, None, None], copied, values)
    bound = 48.0 + float(34000 // KDIM)
    values = jnp.clip(values, -bound, bound)
    return values.reshape(SEQ, HEADS * KDIM).astype(jnp.bfloat16)


def draw_index_query(key, part):
    noise = jax.random.normal(jax.random.fold_in(key, 505), (SEQ, IHEADS, IDIM), jnp.float32)
    values = jnp.clip(noise, -6.0, 6.0) * IDIM ** (-0.5)
    target_score = 120.0 + 200.0 * jax.random.uniform(jax.random.fold_in(key, 506), (SEQ,), jnp.float32)
    factor = target_score / (IDIM * IHEADS * 0.117)
    copied = factor[:, None, None] * index_table(key)[:, None, :]
    values = jnp.where(drawn_flags(key)[:, None, None], copied, values)
    bound = 3.0 + float(60000 // (IDIM * IHEADS))
    values = jnp.clip(values, -bound, bound)
    return values.reshape(SEQ, IHEADS * IDIM).astype(jnp.bfloat16)


def steps_of(stream_key, shape, split, low, largest):
    level, own = 1.0, jax.random.fold_in(stream_key, 6)
    for axis_at, parts in split:
        steps = jnp.exp(jax.random.uniform(jax.random.fold_in(own, axis_at), (parts,), jnp.float32, low / len(split), largest / len(split)))
        level = level * jnp.repeat(steps, shape[axis_at] // parts).reshape([-1 if axis == axis_at else 1 for axis in range(len(shape))])
    return level


def profile(amount, total, reach, skew):
    weights = [(1 << 20) // math.isqrt(rank ** skew) + 1 for rank in range(2, amount + 1)]
    surplus, holding = total - reach - (amount - 1), [1] * (amount - 1)
    while surplus > 0:
        candidates = [i for i in range(amount - 1) if holding[i] < reach]
        mass, left = sum([weights[i] for i in candidates]), surplus
        for i in candidates:
            addition = min(reach - holding[i], max(1, left * weights[i] // mass), surplus)
            holding[i] = holding[i] + addition
            surplus = surplus - addition
    return np.array([reach] + holding)


def ragged_sizes(rng, number_of, total, most, slope):
    if number_of == 2:
        one = jax.random.randint(rng, (), max(1, total - most), min(most, total - 1) + 1)
        return jnp.stack([one, total - one])
    lengths = jnp.asarray(profile(number_of, total, most, slope), jnp.int32)
    couples = (number_of - 1) // 2
    donor, receiver = lengths[1:1 + 2 * couples:2], lengths[2:2 + 2 * couples:2]
    margin = jnp.minimum(donor - 1, most - receiver)
    moved = jax.random.randint(jax.random.fold_in(rng, 1), (couples,), 0, 1 << 20) % (margin + 1)
    lengths = lengths.at[1:1 + 2 * couples:2].set(donor - moved).at[2:2 + 2 * couples:2].set(receiver + moved)
    return lengths[jax.random.permutation(jax.random.fold_in(rng, 2), number_of)]


def setup_inputs(seed: int = 0) -> dict:
    key_of = jax.random.split(jax.random.key(seed), 8)
    return {
        "latent_keys": draw_latent_keys(jax.random.fold_in(key_of[7], 71), 0),
        "index_keys": draw_index_keys(jax.random.fold_in(key_of[7], 71), 0),
        "main_query": draw_main_query(jax.random.fold_in(key_of[7], 71), 0),
        "index_query": draw_index_query(jax.random.fold_in(key_of[7], 71), 0),
        "index_weight": jnp.clip(jnp.exp(math.log(0.29882812) - 2.30176843 * jax.random.uniform(key_of[4], (SEQ, IHEADS), jnp.float32) ** steps_of(key_of[4], (SEQ, IHEADS), ((0, 32), (1, 16)), -0.2, 0.2)), 0.029907227, 0.29882812).astype(jnp.bfloat16),
        "segment_ids": jnp.searchsorted(jnp.cumsum(ragged_sizes(key_of[5], 8, SEQ, SEQ // 4, 2)), jnp.arange(SEQ), side="right").astype(jnp.int32),
        "block_order": jax.random.permutation(key_of[6], 2 * N_CTX).astype(jnp.int32),
    }


score_scale = 192.0 ** -0.5
masked_fill = -1e30


def key_positions(block_order, half_block):
    offsets = jnp.arange(half_block, dtype=jnp.int32)
    return (block_order[:, None] * half_block + offsets[None, :]).reshape(-1).astype(jnp.int32)


def visible_mask(query_pos, key_pos, segment_ids):
    query_seg = jnp.take(segment_ids, query_pos)
    key_seg = jnp.take(segment_ids, key_pos)
    return (key_pos[None, :] <= query_pos[:, None]) & (key_seg[None, :] == query_seg[:, None])


def head_scores(query_head, key_table):
    raw = lax.dot_general(query_head, key_table, (((1,), (1,)), ((), ())), preferred_element_type=jnp.float32)
    return raw * score_scale


def softmax_add(running, scores, visible):
    masked = jnp.where(visible, scores, masked_fill)
    row_max = jnp.max(masked, axis=1, keepdims=True)
    powers = jnp.where(visible, jnp.exp(masked - row_max), 0.0)
    return running + powers / jnp.sum(powers, axis=1, keepdims=True)


def index_scores(query_rows, gains, key_table):
    row_count = query_rows.shape[0]
    head_count = gains.shape[1]
    head_width = query_rows.shape[1] // head_count
    stacked = jnp.moveaxis(query_rows.reshape(row_count, head_count, head_width), 1, 0)
    gain_rows = jnp.moveaxis(gains.astype(jnp.float32), 1, 0)

    def add_head(running, pieces):
        query_head, gain_head = pieces
        dots = lax.dot_general(query_head, key_table, (((1,), (1,)), ((), ())), preferred_element_type=jnp.float32)
        return running + gain_head[:, None] * jnp.maximum(dots, 0.0), None

    start_sum = jnp.zeros((row_count, key_table.shape[0]), jnp.float32)
    running, _ = lax.scan(add_head, start_sum, (stacked, gain_rows))
    return running


def row_terms(target, index_score, visible):
    masked = jnp.where(visible, index_score, masked_fill)
    row_max = jnp.max(masked, axis=1)
    exp_sum = jnp.sum(jnp.where(visible, jnp.exp(masked - row_max[:, None]), 0.0), axis=1)
    positive = target > 0.0
    safe_target = jnp.where(positive, target, 1.0)
    entropy_sum = jnp.sum(jnp.where(positive, target * jnp.log(safe_target), 0.0), axis=1)
    cross_sum = jnp.sum(jnp.where(visible, target * index_score, 0.0), axis=1)
    target_sum = jnp.sum(target, axis=1)
    return row_max, exp_sum, entropy_sum, cross_sum, target_sum


def finish_rows(row_max, exp_sum, entropy_sum, cross_sum, target_sum):
    return entropy_sum - cross_sum + (row_max + jnp.log(exp_sum)) * target_sum


def reference(latent_keys, index_keys, main_query, index_query, index_weight, segment_ids, block_order):
    key_pos = key_positions(block_order, HALF)
    visible = visible_mask(key_pos, key_pos, segment_ids)
    stacked = jnp.moveaxis(main_query.reshape(SEQ, HEADS, KDIM), 1, 0)

    def add_head(running, query_head):
        return softmax_add(running, head_scores(query_head, latent_keys), visible), None

    running, _ = lax.scan(add_head, jnp.zeros((SEQ, SEQ), jnp.float32), stacked)
    target = running / HEADS
    index_score = index_scores(index_query, index_weight, index_keys)
    row_max, exp_sum, entropy_sum, cross_sum, target_sum = row_terms(target, index_score, visible)
    return finish_rows(row_max, exp_sum, entropy_sum, cross_sum, target_sum)
```

```python
import functools
import math

import jax
import jax.numpy as jnp
from jax import lax
from jax.experimental import pallas as pl
from jax.experimental.pallas import tpu as pltpu
from jax.sharding import PartitionSpec as P

HEADS = 128
HALF = 64
FILL = -1e30
EXP_SCALE = 192.0 ** (-0.5) * math.log2(math.e)
MESH = pl.DeviceIdType.MESH
NT = (((1,), (1,)), ((), ()))
F32 = jnp.float32


def dot_nt(a, b):
    return lax.dot_general(a, b, NT, preferred_element_type=F32)


def fused(
    ny, nh, reach, share, heads, iheads,
    slots_ref, lat_in, idx_in, mq_ref, iq_ref, gain_ref, info_ref,
    out_ref,
    lat, idx, mq, iq, win, iwin, score, total, iscore, trecv, irecv, stats, srecv,
    snd, rcv, xsend, xrecv,
):
    kdim = lat_in.shape[1]
    rows_w = nh * share
    me_c, me_h = lax.axis_index("ctx"), lax.axis_index("head")
    core = me_c % 2
    y = (me_c // 2) % ny
    xl = me_c // (2 * ny)
    xh = me_h % 2
    far = ny // 2

    def ctx_of(xl_, y_, core_):
        return (xl_ * ny + y_) * 2 + core_

    up = (ctx_of(xl, (y + 1) % ny, core), me_h)
    down = (ctx_of(xl, (y + ny - 1) % ny, core), me_h)
    cross = (
        (ctx_of(1 - xl, y, core), me_h),
        (ctx_of(1 - xl, y, core), me_h - xh + (1 - xh)),
    )
    sibling = (ctx_of(xl, y, 1 - core), me_h)

    barrier = pltpu.get_barrier_semaphore()
    for dev in (up, down, cross[0], cross[1], sibling):
        pl.semaphore_signal(barrier, inc=1, device_id=dev, device_id_type=MESH)

    def greet(i, _):
        pl.semaphore_signal(
            barrier, inc=1, device_id=(me_c, (me_h + i) % nh), device_id_type=MESH
        )
        return 0

    lax.fori_loop(1, nh, greet, 0)

    own = ctx_of(xl, y, core)
    for h in (0, 1):
        idx[own * 2 + h] = idx_in[h * HALF:(h + 1) * HALF, :]
        lat[own * 2 + h] = lat_in[h * HALF:(h + 1) * HALF, :]

    pl.semaphore_wait(barrier, 5 + nh - 1)

    bufs = (idx, lat)
    started = []

    def send(b, slot, dev, lane):
        copy = pltpu.make_async_remote_copy(
            src_ref=bufs[b].at[slot], dst_ref=bufs[b].at[slot],
            send_sem=snd.at[b, lane], recv_sem=rcv.at[b, slot],
            device_id=dev, device_id_type=MESH,
        )
        copy.start()
        started.append(copy)

    def await_slot(b, slot):
        pltpu.make_async_remote_copy(
            src_ref=bufs[b].at[slot], dst_ref=bufs[b].at[slot],
            send_sem=snd.at[b, 0], recv_sem=rcv.at[b, slot],
            device_id=sibling, device_id_type=MESH,
        ).wait_recv()

    lanes = [0, 0]

    def lane(b):
        lanes[b] += 1
        return lanes[b] - 1

    def goes(dist, h, way):
        return dist < far or (dist == far and h == way)

    def ring_step(b, s):
        for h in (0, 1):
            for way in (0, 1):
                if s == 0 and way == 1:
                    continue
                if s > 0 and not goes(s, h, way):
                    continue
                yy = (y + ny - s) % ny if way == 0 else (y + s) % ny
                slot = ctx_of(xl, yy, core) * 2 + h
                if s > 0:
                    await_slot(b, slot)
                for w in ((0, 1) if s == 0 else (way,)):
                    if goes(s + 1, h, w):
                        send(b, slot, up if w == 0 else down, lane(b))
                send(b, slot, cross[h], lane(b))
                send(b, slot, sibling, lane(b))

    def cross_step(b, s):
        for h in (0, 1):
            for way in (0, 1):
                if s == 0 and way == 1:
                    continue
                if s > 0 and not goes(s, h, way):
                    continue
                yy = (y + ny - s) % ny if way == 0 else (y + s) % ny
                slot = ctx_of(1 - xl, yy, core) * 2 + h
                await_slot(b, slot)
                send(b, slot, sibling, lane(b))

    def sibling_wait(b):
        for xx in (0, 1):
            for yy in range(ny):
                for h in (0, 1):
                    await_slot(b, ctx_of(xx, yy, 1 - core) * 2 + h)

    def prepare():
        for qb in (0, 1):
            rows = slice(qb * HALF, (qb + 1) * HALF)
            for h in range(heads):
                mq[qb, h * HALF:(h + 1) * HALF, :] = mq_ref[rows, h * kdim:(h + 1) * kdim]
            for h in range(iheads):
                iq[qb, h * HALF:(h + 1) * HALF, :] = iq_ref[rows, h * 128:(h + 1) * 128]
        pad = rows_w - reach * HALF
        if pad:
            for qb in (0, 1):
                win[qb, reach * HALF:, :] = jnp.zeros((pad, kdim), jnp.bfloat16)
                iwin[qb, reach * HALF:, :] = jnp.zeros((pad, 128), jnp.bfloat16)

    def seen(which, first, count):
        kp = info_ref[which, 2:3, :] + first + lax.broadcasted_iota(jnp.int32, (count, 128), 0)
        return (kp >= info_ref[which, 0:1, :]) & (kp <= info_ref[which, 1:2, :])

    groups = 4
    size = rows_w // groups

    def left_of(count):
        return lax.broadcasted_iota(jnp.int32, (count, 128), 1) < HALF

    def part(g):
        return pl.ds(pl.multiple_of(g * size, 16), size)

    def fill(dst, src, qb):
        def body(j, _):
            at = pl.ds(pl.multiple_of(j * HALF, HALF), HALF)
            dst[qb, at, :] = src[slots_ref[qb * reach + j]]
            return 0
        lax.fori_loop(0, reach, body, 0)

    def chunk(d):
        return pl.ds(pl.multiple_of(d * share, 8), share)

    def fold(x):
        part = x[:, 0:128]
        for i in range(1, x.shape[1] // 128):
            part = part + x[:, i * 128:(i + 1) * 128]
        return part + pltpu.roll(part, HALF, 1)

    def exchange(kind, src, dst, i, start):
        to = (me_h + i) % nh
        frm = (me_h + nh - i) % nh
        there = src.at[chunk(to), :] if kind < 2 else src
        copy = pltpu.make_async_remote_copy(
            src_ref=there, dst_ref=dst.at[me_h] if start else dst.at[frm],
            send_sem=xsend.at[kind, to],
            recv_sem=xrecv.at[kind, me_h] if start else xrecv.at[kind, frm],
            device_id=(me_c, to), device_id_type=MESH,
        )
        if start:
            copy.start()
        else:
            copy.wait()
        return 0

    def index_part():
        for qb in (0, 1):
            fill(iwin, idx, qb)

        def body(d, _):
            pair = []
            for qb in (0, 1):
                dots = dot_nt(iwin[qb, part(d), :], iq[qb])
                pair.append(fold(jnp.maximum(dots, 0.0) * gain_ref[qb:qb + 1, :]))
            iscore[part(d), :] = jnp.where(left_of(size), pair[0], pair[1])
            return 0

        lax.fori_loop(0, groups, body, 0)
        lax.fori_loop(1, nh, lambda i, _: exchange(0, iscore, irecv, i, True), 0)

    def main_part():
        wide = heads * HALF
        inverses, tops = [], []
        for qb in (0, 1):
            fill(win, lat, qb)

            def first(g, top, qb=qb):
                at = part(g)
                s = dot_nt(win[qb, at, :], mq[qb])
                bias = jnp.where(seen(qb, g * size, size), 0.0, FILL)
                s = s + jnp.concatenate([bias] * (wide // 128), axis=1)
                score[qb, at, :] = s
                return jnp.maximum(top, jnp.max(s.reshape(size // 8, 8, wide), axis=0))

            top = lax.fori_loop(0, groups, first, jnp.full((8, wide), FILL, F32))
            top = jnp.max(top, axis=0, keepdims=True)

            def second(g, acc, qb=qb, top=top):
                p = jnp.exp2((score[qb, chunk(g), :] - top) * EXP_SCALE)
                score[qb, chunk(g), :] = p
                return acc + jnp.sum(p.reshape(share // 8, 8, wide), axis=0)

            acc = lax.fori_loop(0, nh, second, jnp.zeros((8, wide), F32))
            inverses.append(1.0 / jnp.sum(acc, axis=0, keepdims=True))

        def third(i, _):
            d = (me_h + i) % nh
            pair = [fold(score[qb, chunk(d), :] * inverses[qb]) for qb in (0, 1)]
            total[chunk(d), :] = jnp.where(left_of(share), pair[0], pair[1])

            @pl.when(i < nh)
            def _():
                exchange(1, total, trecv, i, True)

            return 0

        lax.fori_loop(1, nh + 1, third, 0)

    def gathered_sum(kind, src, dst):
        def body(i, acc):
            exchange(kind, src, dst, i, False)
            return acc + dst[(me_h + nh - i) % nh]
        return lax.fori_loop(1, nh, body, src[chunk(me_h), :])

    ring_step(0, 0)
    ring_step(1, 0)
    prepare()
    for s in range(1, far + 1):
        ring_step(0, s)
        cross_step(0, s - 1)
        if s % 2 == 0:
            ring_step(1, s // 2)
            cross_step(1, s // 2 - 1)
    cross_step(0, far)
    done = far // 2
    for s in range(done + 1, far):
        ring_step(1, s)
        cross_step(1, s - 1)
    sibling_wait(0)
    index_part()
    for s in range(max(far, done + 1), far + 1):
        ring_step(1, s)
        cross_step(1, s - 1)
    cross_step(1, far)
    sibling_wait(1)
    main_part()

    vis = seen(2, me_h * share, share)
    index_score = gathered_sum(0, iscore, irecv)
    masked = jnp.where(vis, index_score, FILL)
    top = jnp.max(masked, axis=0, keepdims=True)
    exp_sum = jnp.sum(jnp.where(vis, jnp.exp(masked - top), 0.0), axis=0, keepdims=True)
    target = gathered_sum(1, total, trecv) * (1.0 / HEADS)
    positive = target > 0.0
    logs = jnp.log(jnp.where(positive, target, 1.0))
    gain = jnp.sum(
        jnp.where(positive, target * logs, 0.0) - jnp.where(vis, target * index_score, 0.0),
        axis=0, keepdims=True,
    )
    mass = jnp.sum(target, axis=0, keepdims=True)
    stats[0:1, :] = top
    stats[1:2, :] = exp_sum
    stats[2:3, :] = gain
    stats[3:4, :] = mass
    stats[4:8, :] = jnp.zeros((4, 128), F32)
    lax.fori_loop(1, nh, lambda i, _: exchange(2, stats, srecv, i, True), 0)
    srecv[me_h] = stats[...]
    lax.fori_loop(1, nh, lambda i, _: exchange(2, stats, srecv, i, False), 0)
    every = srecv[...]
    tops = every[:, 0:1, :]
    peak = jnp.max(tops, axis=0, keepdims=True)
    exp_all = jnp.sum(every[:, 1:2, :] * jnp.exp(tops - peak), axis=0)
    gain_all = jnp.sum(every[:, 2:3, :], axis=0)
    mass_all = jnp.sum(every[:, 3:4, :], axis=0)
    out_ref[...] = gain_all + (peak[0] + jnp.log(exp_all)) * mass_all
    for copy in started:
        copy.wait_send()


def per_device(
    latent_keys, index_keys, main_query, index_query, index_weight, segment_ids, block_order
):
    rows, kdim = latent_keys.shape
    nc, nh = lax.axis_size("ctx"), lax.axis_size("head")
    ny = nc // 4
    blocks = 2 * nc
    reach = nc // 2 + 1
    heads = main_query.shape[1] // kdim
    iheads = index_weight.shape[1]
    share = -(-reach * HALF // (8 * nh)) * 8
    ids = jnp.arange(blocks, dtype=jnp.int32)
    mine = lax.dynamic_slice_in_dim(block_order, lax.axis_index("ctx") * 2, 2)
    wanted = jnp.maximum(
        mine[:, None] - (reach - 1) + jnp.arange(reach, dtype=jnp.int32)[None, :], 0
    ).reshape(-1)
    slots = jnp.sum(
        jnp.where(block_order[None, :] == wanted[:, None], ids[None, :], 0), axis=1
    )
    pos = (mine[:, None] * HALF + jnp.arange(HALF, dtype=jnp.int32)[None, :]).reshape(-1)
    seg = jnp.take(segment_ids, pos)
    start = jnp.sum((segment_ids[None, :] < seg[:, None]).astype(jnp.int32), axis=1)
    base = jnp.repeat(mine - (reach - 1), HALF) * HALF
    info = jnp.stack([start, pos, base])
    info = jnp.pad(info, ((0, 5), (0, 0)))
    a, b = info[:, :HALF], info[:, HALF:]
    info = jnp.stack(
        [jnp.concatenate([a, a], 1), jnp.concatenate([b, b], 1), info]
    )
    gains = index_weight.astype(F32).reshape(2, HALF, iheads)
    gains = jnp.moveaxis(gains, 2, 1).reshape(2, iheads * HALF)

    rows_w = nh * share
    wide = heads * HALF
    bf = jnp.bfloat16
    vmem = pl.BlockSpec(memory_space=pltpu.VMEM)
    lanes = 14 + 16 + 32
    out = pl.pallas_call(
        functools.partial(fused, ny, nh, reach, share, heads, iheads),
        out_shape=jax.ShapeDtypeStruct((1, rows), F32),
        in_specs=[pl.BlockSpec(memory_space=pltpu.SMEM)] + [vmem] * 6,
        out_specs=vmem,
        scratch_shapes=[
            pltpu.VMEM((blocks, HALF, kdim), bf),
            pltpu.VMEM((blocks, HALF, 128), bf),
            pltpu.VMEM((2, wide, kdim), bf),
            pltpu.VMEM((2, iheads * HALF, 128), bf),
            pltpu.VMEM((2, rows_w, kdim), bf),
            pltpu.VMEM((2, rows_w, 128), bf),
            pltpu.VMEM((2, rows_w, wide), F32),
            pltpu.VMEM((rows_w, 128), F32),
            pltpu.VMEM((rows_w, 128), F32),
            pltpu.VMEM((nh, share, 128), F32),
            pltpu.VMEM((nh, share, 128), F32),
            pltpu.VMEM((8, 128), F32),
            pltpu.VMEM((nh, 8, 128), F32),
            pltpu.SemaphoreType.DMA((2, lanes)),
            pltpu.SemaphoreType.DMA((2, blocks)),
            pltpu.SemaphoreType.DMA((3, nh)),
            pltpu.SemaphoreType.DMA((3, nh)),
        ],
        compiler_params=pltpu.CompilerParams(
            collective_id=0, has_side_effects=True, vmem_limit_bytes=56 * 2**20
        ),
    )(slots, latent_keys, index_keys, main_query, index_query, gains, info)
    return out.reshape(rows)


def solution(mesh):
    in_specs = (
        P("ctx", None),
        P("ctx", None),
        P("ctx", "head"),
        P("ctx", "head"),
        P("ctx", "head"),
        P(),
        P(),
    )
    return jax.shard_map(
        per_device, mesh=mesh, in_specs=in_specs, out_specs=P("ctx"), check_vma=False
    )
```

```python
import functools
import math

import jax
import jax.numpy as jnp
from jax import lax
from jax.experimental import pallas as pl
from jax.experimental.pallas import tpu as pltpu
from jax.sharding import PartitionSpec as P

HEADS = 128
HALF = 64
LAT = 512
ROPE = 64
FILL = -1e30
EXP_SCALE = 192.0 ** (-0.5) * math.log2(math.e)
MESH = pl.DeviceIdType.MESH
NT = (((1,), (1,)), ((), ()))
F32 = jnp.float32
BF16 = jnp.bfloat16
GROUP = 4
PAD_J = 24
FOLD = 640


def dot_nt(a, b):
    return lax.dot_general(a, b, NT, preferred_element_type=F32)


def total_of(x):
    return jnp.sum(jnp.sum(x, axis=1, keepdims=True), axis=0, keepdims=True)


def fused(
    ny, nh, reach, heads, iheads,
    lat_in, idx_in, mq_hbm, iq_in, gain_in, seg_in, order_in,
    out_ref,
    lat, idx, mraw, mq, score, bias, iq_send, iq_recv, ilhs, iwide, ipack,
    slot_v, slot_s, tsend, trecv, town, fsend, frecv,
    snd, rcv, lrcv, xsend, xrecv, local, token,
):
    kdim = LAT + ROPE
    me_c, me_h = lax.axis_index("ctx"), lax.axis_index("head")
    core = me_c % 2
    y = (me_c // 2) % ny
    xl = me_c // (2 * ny)
    xh = me_h % 2
    z = me_h // 2
    nz = nh // 2
    far = ny // 2
    half_h = nh // 2
    width = -(-reach * HALF // 128) * 128

    def ctx_of(xl_, y_, core_):
        return (xl_ * ny + y_) * 2 + core_

    up = (ctx_of(xl, (y + 1) % ny, core), me_h)
    down = (ctx_of(xl, (y + ny - 1) % ny, core), me_h)
    cross = (
        (ctx_of(1 - xl, y, core), me_h),
        (ctx_of(1 - xl, y, core), z * 2 + 1 - xh),
    )
    sibling = (ctx_of(xl, y, 1 - core), me_h)
    zup = (me_c, ((z + 1) % nz) * 2 + xh)
    zdown = (me_c, ((z + nz - 1) % nz) * 2 + xh)
    twin = (me_c, z * 2 + 1 - xh)
    near = (up, down, cross[0], cross[1], sibling, zup, zdown, twin)

    mq_copy = pltpu.make_async_copy(mq_hbm, mraw, local.at[0])
    mq_copy.start()
    barrier = pltpu.get_barrier_semaphore()
    for dev in near:
        pl.semaphore_signal(barrier, inc=1, device_id=dev, device_id_type=MESH)

    own = ctx_of(xl, y, core)
    keys = jnp.transpose(lat_in[...])
    lat[own, :, 0:LAT] = keys[0:HALF, 0:LAT]
    lat[own, :, LAT:2 * LAT] = keys[HALF:, 0:LAT]
    lat[own, :, 2 * LAT:] = jnp.concatenate([keys[0:HALF, LAT:], keys[HALF:, LAT:]], axis=1)
    for h in (0, 1):
        idx[own * 2 + h] = idx_in[h * HALF:(h + 1) * HALF, :]

    pl.semaphore_wait(barrier, len(near))

    started = []
    lanes = [0]

    def piece(b, c, h):
        if b == 0:
            return idx.at[c * 2 + h], rcv.at[c * 2 + h]
        return lat.at[c, pl.ds(h * (HALF // 2), HALF // 2)], lrcv.at[c * 2 + h]

    def send(b, c, h, dev):
        ref, sem = piece(b, c, h)
        copy = pltpu.make_async_remote_copy(
            src_ref=ref, dst_ref=ref, send_sem=snd.at[lanes[0]], recv_sem=sem,
            device_id=dev, device_id_type=MESH,
        )
        lanes[0] += 1
        copy.start()
        started.append(copy)

    def arrived(b, c, h):
        ref, sem = piece(b, c, h)
        pltpu.make_async_remote_copy(
            src_ref=ref, dst_ref=ref, send_sem=snd.at[0], recv_sem=sem,
            device_id=sibling, device_id_type=MESH,
        ).wait_recv()

    def goes(dist, h, way):
        return dist < far or (dist == far and h == way)

    def visits(s):
        for h in (0, 1):
            for way in (0, 1):
                if s == 0 and way == 1:
                    continue
                if s > 0 and not goes(s, h, way):
                    continue
                yield h, way, (y + ny - s) % ny if way == 0 else (y + s) % ny

    def ring_step(b, s):
        for h, way, yy in visits(s):
            c = ctx_of(xl, yy, core)
            if s > 0:
                arrived(b, c, h)
            for w in ((0, 1) if s == 0 else (way,)):
                if goes(s + 1, h, w):
                    send(b, c, h, up if w == 0 else down)
            send(b, c, h, cross[h])
            send(b, c, h, sibling)

    def cross_step(b, s):
        for h, way, yy in visits(s):
            c = ctx_of(1 - xl, yy, core)
            arrived(b, c, h)
            send(b, c, h, sibling)

    def sibling_wait(b):
        for xx in (0, 1):
            for yy in range(ny):
                for h in (0, 1):
                    arrived(b, ctx_of(xx, yy, 1 - core), h)

    def token_signal():
        pl.semaphore_signal(token.at[0], inc=1, device_id=zup, device_id_type=MESH)
        pl.semaphore_signal(token.at[1], inc=1, device_id=zdown, device_id_type=MESH)

    def token_wait():
        pl.semaphore_wait(token.at[0], 1)
        pl.semaphore_wait(token.at[1], 1)

    def exchange(kind, src, dst, i, start):
        to = (me_h + i) % nh
        frm = (me_h + nh - i) % nh
        copy = pltpu.make_async_remote_copy(
            src_ref=src(to), dst_ref=dst.at[me_h] if start else dst.at[frm],
            send_sem=xsend.at[kind, to],
            recv_sem=xrecv.at[kind, me_h] if start else xrecv.at[kind, frm],
            device_id=(me_c, to), device_id_type=MESH,
        )
        if start:
            copy.start()
        else:
            copy.wait()
        return 0

    def prepare_small():
        gains = jnp.concatenate(
            [gain_in[...].astype(F32), jnp.zeros((128 - iheads, 128), F32)], axis=0
        )
        gains = jnp.transpose(gains).astype(BF16)
        for i in range(8):
            rows = slice(16 * i, 16 * i + 16)
            iq_send[i, :, 0:iheads * 128] = iq_in[rows, :]
            iq_send[i, :, iheads * 128:] = gains[rows, :]
        order = order_in[...]
        blocks = order.shape[1]
        lane = lax.broadcasted_iota(jnp.int32, (1, blocks), 1)
        segs = seg_in[...].astype(F32)
        seg_row = lax.broadcasted_iota(jnp.int32, segs.shape, 0).astype(F32)
        counts = [total_of(jnp.where(segs == float(v), 1.0, 0.0)) for v in range(7)]
        for qb in (0, 1):
            mine_i = jnp.sum(jnp.where(lane == 2 * me_c + qb, order, 0), axis=1, keepdims=True)
            j = lax.broadcasted_iota(jnp.int32, (PAD_J, blocks), 0)
            want = jnp.maximum(mine_i - (reach - 1) + j, 0)
            at = lax.broadcasted_iota(jnp.int32, (PAD_J, blocks), 1)
            slot = jnp.sum(jnp.where(order == want, at, 0), axis=1, keepdims=True)
            slot = jnp.minimum(slot, blocks - 1)
            slot = jnp.broadcast_to(slot, (PAD_J, 128))
            slot_v[0, qb * PAD_J:(qb + 1) * PAD_J, :] = slot
            slot_v[1, qb * PAD_J:(qb + 1) * PAD_J, :] = slot >> 1
            slot_v[2, qb * PAD_J:(qb + 1) * PAD_J, :] = slot & 1
            mine = mine_i.astype(F32)
            first = mine - float(reach - 1)
            pair = jnp.floor(mine * 0.5)
            row = jnp.sum(jnp.where(seg_row == pair, segs, 0.0), axis=0, keepdims=True)
            row = jnp.where(mine - 2.0 * pair > 0.5, pltpu.roll(row, HALF, 1), row)
            sub = lax.broadcasted_iota(jnp.int32, (HALF, 128), 0)
            lan = lax.broadcasted_iota(jnp.int32, (HALF, 128), 1)
            seg_q = jnp.sum(jnp.where(sub == lan, row, 0.0), axis=1, keepdims=True)
            start = jnp.zeros((HALF, 1), F32)
            for v in range(7):
                start = start + jnp.where(seg_q > float(v), counts[v], 0.0)
            pos = mine * float(HALF) + lax.broadcasted_iota(
                jnp.int32, (HALF, 1), 0
            ).astype(F32)
            kp = first * float(HALF) + lax.broadcasted_iota(
                jnp.int32, (HALF, width), 1
            ).astype(F32)
            bias[qb] = jnp.where((kp >= start) & (kp <= pos), 0.0, FILL)
        copy = pltpu.make_async_copy(slot_v, slot_s, local.at[1])
        copy.start()
        copy.wait()

    def prepare_queries():
        mq_copy.wait()
        for qb in (0, 1):
            for slab in range(4):
                rows = slice(qb * HALF + slab * 16, qb * HALF + slab * 16 + 16)
                for h in range(heads):
                    x = mraw[rows, h * kdim:(h + 1) * kdim]
                    at = slab * 16 * heads + h * 16
                    mq[qb, at:at + 16, 0:LAT] = x[:, 0:LAT]
                    mq[qb, at:at + 16, LAT:] = jnp.concatenate([x[:, LAT:], x[:, LAT:]], axis=1)

    def index_queries():
        def body(i, _):
            exchange(0, lambda to: iq_send.at[to // 2], iq_recv, i, False)
            return 0
        lax.fori_loop(1, nh, body, 0)
        iq_recv[me_h] = iq_send[me_h // 2]
        odd = me_h % 2

        def pick(s, _):
            x = iq_recv[s].astype(F32)
            x = jnp.where(odd == 0, x[0:8], x[8:16])
            at = pl.multiple_of(s * iheads * 8, 16)
            ilhs[pl.ds(at, iheads * 8), :] = jnp.concatenate(
                [x[:, k * 128:(k + 1) * 128] for k in range(iheads)], axis=0
            ).astype(BF16)
            g = x[:, iheads * 128:]
            iwide[pl.ds(at, iheads * 8), :] = jnp.concatenate(
                [jnp.broadcast_to(g[:, k:k + 1], (8, 128)) for k in range(iheads)], axis=0
            )
            return 0

        lax.fori_loop(0, nh, pick, 0)

    mine_qb = me_h // half_h
    mine_row = (me_h % half_h) * 8

    def index_scores():
        rows = ilhs.shape[0]

        def scores(first, count, at):
            ks = [idx[slot_s[0, mine_qb * PAD_J + first + k, 0]] for k in range(count)]
            ks += ks[-1:] * (-count % 2)
            dots = dot_nt(ilhs[...], jnp.concatenate(ks, axis=0))
            for k in range(dots.shape[1] // 128):
                part = jnp.maximum(dots[:, k * 128:(k + 1) * 128], 0.0) * iwide[...]
                part = jnp.sum(part.reshape(rows // 8, 8, 128), axis=0)
                lo = at + k * 128
                if lo < FOLD:
                    ipack[0:8, lo:lo + 128] = part
                else:
                    ipack[8:16, lo - FOLD:lo - FOLD + 128] = part

        for first in range(0, reach, GROUP):
            scores(first, min(GROUP, reach - first), first * HALF)
        ipack[8:16, width - FOLD:] = jnp.zeros((8, 2 * FOLD - width), F32)

    def packed_bias():
        b = bias[mine_qb, pl.ds(pl.multiple_of(mine_row, 8), 8), :]
        rest = jnp.full((8, 2 * FOLD - width), FILL, F32)
        return jnp.concatenate(
            [b[:, 0:FOLD], jnp.concatenate([b[:, FOLD:], rest], axis=1)], axis=0
        )

    def both(x, op):
        return op(x[0:8], x[8:16])

    def key_block(qb, j):
        rows = lat[slot_s[1, qb * PAD_J + j, 0]]
        odd = slot_s[2, qb * PAD_J + j, 0]
        lane = lax.broadcasted_iota(jnp.int32, (HALF, 128), 1)
        second = lane * 0 + odd > 0
        second = jnp.concatenate([second] * (LAT // 128), axis=1)
        main = jnp.where(second, rows[:, LAT:2 * LAT], rows[:, 0:LAT])
        tail = rows[:, 2 * LAT:]
        tail = jnp.where(lane // HALF == odd, tail, jnp.zeros_like(tail))
        return jnp.concatenate([main, tail], axis=1)

    def scores_of(qb):
        def body(g, _):
            ks = jnp.concatenate([key_block(qb, g * GROUP + k) for k in range(GROUP)], axis=0)
            at = pl.ds(pl.multiple_of(g * GROUP * HALF, 256), GROUP * HALF)
            score[:, at] = dot_nt(mq[qb], ks)
            return 0

        lax.fori_loop(0, reach // GROUP, body, 0)
        left = reach % GROUP
        ks = [key_block(qb, reach - left + k) for k in range(left)]
        ks += ks[-1:] * (-left % 2)
        score[:, (reach - left) * HALF:] = dot_nt(mq[qb], jnp.concatenate(ks, axis=0))

    def shares_of(qb):
        def body(i, _):
            g = (me_h + i) % half_h
            d = qb * half_h + g
            b = bias[qb, pl.ds(pl.multiple_of(g * 8, 8), 8), :]
            base = (g // 2) * (16 * heads) + (g % 2) * 8
            acc = jnp.zeros((8, width), F32)
            for h in range(heads):
                s = score[pl.ds(pl.multiple_of(base + h * 16, 8), 8), :] + b
                top = jnp.max(s, axis=1, keepdims=True)
                p = jnp.exp2((s - top) * EXP_SCALE)
                acc = acc + p * (1.0 / jnp.sum(p, axis=1, keepdims=True))
            rest = jnp.zeros((8, 2 * FOLD - width), F32)
            packed = jnp.concatenate(
                [acc[:, 0:FOLD], jnp.concatenate([acc[:, FOLD:], rest], axis=1)], axis=0
            )
            tsend[d] = packed.astype(BF16)

            @pl.when(d == me_h)
            def _():
                town[...] = packed

            @pl.when(d != me_h)
            def _():
                pltpu.make_async_remote_copy(
                    src_ref=tsend.at[d], dst_ref=trecv.at[me_h],
                    send_sem=xsend.at[1, d], recv_sem=xrecv.at[1, me_h],
                    device_id=(me_c, d), device_id_type=MESH,
                ).start()

            return 0

        lax.fori_loop(1, half_h + 1, body, 0)

    ring_step(0, 0)
    ring_step(1, 0)
    token_signal()
    prepare_small()
    rounds = nz // 2
    token_wait()
    done = 1
    if done < rounds:
        token_signal()
    prepare_queries()
    for s in range(1, far + 1):
        ring_step(0, s)
        ring_step(1, s)
        for b in (0, 1):
            if done < rounds:
                token_wait()
                done += 1
                if done < rounds:
                    token_signal()
            elif done == rounds:
                lax.fori_loop(
                    1, nh,
                    lambda i, _: exchange(0, lambda to: iq_send.at[to // 2], iq_recv, i, True), 0,
                )
                done += 1
            cross_step(b, s - 1)
    index_queries()
    cross_step(0, far)
    cross_step(1, far)
    sibling_wait(0)
    index_scores()
    seen_bias = packed_bias()
    index_score = ipack[...]
    masked = index_score + seen_bias
    top = both(jnp.max(masked, axis=1, keepdims=True), jnp.maximum)
    tops = jnp.concatenate([top, top], axis=0)
    exp_sum = both(jnp.sum(jnp.exp(masked - tops), axis=1, keepdims=True), jnp.add)
    lse = top + jnp.log(exp_sum)
    sibling_wait(1)

    for qb in (0, 1):
        scores_of(qb)
        shares_of(qb)

    def add_share(i, acc):
        exchange(1, lambda to: tsend.at[to], trecv, i, False)
        return acc + trecv[(me_h + nh - i) % nh].astype(F32)

    target = lax.fori_loop(1, nh, add_share, town[...]) * (1.0 / HEADS)
    positive = target > 0.0
    logs = jnp.log(jnp.where(positive, target, 1.0))
    gain = both(
        jnp.sum(target * (logs - index_score), axis=1, keepdims=True), jnp.add
    )
    mass = both(jnp.sum(target, axis=1, keepdims=True), jnp.add)
    kl = gain + lse * mass + (1.0 - mass)
    sub = lax.broadcasted_iota(jnp.int32, (8, 128), 0)
    lan = lax.broadcasted_iota(jnp.int32, (8, 128), 1)
    mine = jnp.where(lan == 8 * me_h + sub, kl, 0.0)
    fsend[...] = mine
    lax.fori_loop(1, nh, lambda i, _: exchange(2, lambda to: fsend, frecv, i, True), 0)
    frecv[me_h] = mine
    for copy in started:
        copy.wait_send()
    lax.fori_loop(1, nh, lambda i, _: exchange(2, lambda to: fsend, frecv, i, False), 0)
    out_ref[...] = jnp.sum(jnp.sum(frecv[...], axis=0), axis=0, keepdims=True)


def per_device(
    latent_keys, index_keys, main_query, index_query, index_weight, segment_ids, block_order
):
    rows, kdim = latent_keys.shape
    nc, nh = lax.axis_size("ctx"), lax.axis_size("head")
    ny = nc // 4
    blocks = 2 * nc
    reach = nc // 2 + 1
    heads = main_query.shape[1] // kdim
    iheads = index_weight.shape[1]
    width = -(-reach * HALF // 128) * 128
    wide = heads * HALF
    vmem = pl.BlockSpec(memory_space=pltpu.VMEM)
    hbm = pl.BlockSpec(memory_space=pl.ANY)
    dma = pltpu.SemaphoreType.DMA
    out = pl.pallas_call(
        functools.partial(fused, ny, nh, reach, heads, iheads),
        out_shape=jax.ShapeDtypeStruct((1, rows), F32),
        in_specs=[vmem, vmem, hbm, vmem, vmem, vmem, vmem],
        out_specs=vmem,
        scratch_shapes=[
            pltpu.VMEM((nc, HALF, 2 * kdim), BF16),
            pltpu.VMEM((blocks, HALF, 128), BF16),
            pltpu.VMEM((rows, heads * kdim), BF16),
            pltpu.VMEM((2, wide, LAT + 2 * ROPE), BF16),
            pltpu.VMEM((wide, width), F32),
            pltpu.VMEM((2, HALF, width), F32),
            pltpu.VMEM((8, 16, iheads * 128 + 128), BF16),
            pltpu.VMEM((nh, 16, iheads * 128 + 128), BF16),
            pltpu.VMEM((nh * iheads * 8, 128), BF16),
            pltpu.VMEM((nh * iheads * 8, 128), F32),
            pltpu.VMEM((16, FOLD), F32),
            pltpu.VMEM((3, 2 * PAD_J, 128), jnp.int32),
            pltpu.SMEM((3, 2 * PAD_J, 128), jnp.int32),
            pltpu.VMEM((nh, 16, FOLD), BF16),
            pltpu.VMEM((nh, 16, FOLD), BF16),
            pltpu.VMEM((16, FOLD), F32),
            pltpu.VMEM((8, 128), F32),
            pltpu.VMEM((nh, 8, 128), F32),
            dma((4 * (7 * ny + 4),)),
            dma((blocks,)),
            dma((blocks,)),
            dma((3, nh)),
            dma((3, nh)),
            dma((2,)),
            pltpu.SemaphoreType.REGULAR((2,)),
        ],
        compiler_params=pltpu.CompilerParams(
            collective_id=0, has_side_effects=True, vmem_limit_bytes=48 * 2**20
        ),
    )(
        latent_keys.T, index_keys, main_query, index_query, index_weight.T,
        segment_ids.reshape(-1, 128), block_order.reshape(1, blocks),
    )
    return out.reshape(rows)


def solution(mesh):
    in_specs = (
        P("ctx", None),
        P("ctx", None),
        P("ctx", "head"),
        P("ctx", "head"),
        P("ctx", "head"),
        P(),
        P(),
    )
    return jax.shard_map(
        per_device, mesh=mesh, in_specs=in_specs, out_specs=P("ctx"), check_vma=False
    )
```

```python
import functools
import math

import jax
import jax.numpy as jnp
from jax import lax
from jax.experimental import pallas as pl
from jax.experimental.pallas import tpu as pltpu
from jax.sharding import PartitionSpec as P

HEADS = 128
HALF = 64
LAT = 512
ROPE = 64
FILL = -1e30
EXP_SCALE = 192.0 ** (-0.5) * math.log2(math.e)
MESH = pl.DeviceIdType.MESH
NT = (((1,), (1,)), ((), ()))
F32 = jnp.float32
BF16 = jnp.bfloat16
GROUP = 4
PAD_J = 24


def dot_nt(a, b):
    return lax.dot_general(a, b, NT, preferred_element_type=F32)


def total_of(x):
    return jnp.sum(jnp.sum(x, axis=1, keepdims=True), axis=0, keepdims=True)


def fused(
    ny, nh, reach, heads, iheads,
    lat_hbm, idx_hbm, mq_hbm, iq_hbm, gain_hbm, seg_hbm, order_hbm,
    out_ref,
    lat_in, idx_in, iq_in, gain_in, seg_in, order_in,
    lat, idx, mraw, mq, score, bias, iq_send, iq_recv, ilhs, iwide, ipack,
    slot_v, slot_s, tsend, trecv, town, fsend, frecv,
    snd, rcv, lrcv, xsend, xrecv, local, token,
):
    kdim = LAT + ROPE
    me_c, me_h = lax.axis_index("ctx"), lax.axis_index("head")
    core = me_c % 2
    y = (me_c // 2) % ny
    xl = me_c // (2 * ny)
    xh = me_h % 2
    z = me_h // 2
    nz = nh // 2
    far = ny // 2
    half_h = nh // 2
    width = (reach - 1) * HALF
    fold = width // 2

    def ctx_of(xl_, y_, core_):
        return (xl_ * ny + y_) * 2 + core_

    up = (ctx_of(xl, (y + 1) % ny, core), me_h)
    down = (ctx_of(xl, (y + ny - 1) % ny, core), me_h)
    cross = (
        (ctx_of(1 - xl, y, core), me_h),
        (ctx_of(1 - xl, y, core), z * 2 + 1 - xh),
    )
    sibling = (ctx_of(xl, y, 1 - core), me_h)
    zup = (me_c, ((z + 1) % nz) * 2 + xh)
    zdown = (me_c, ((z + nz - 1) % nz) * 2 + xh)
    twin = (me_c, z * 2 + 1 - xh)
    near = (up, down, cross[0], cross[1], sibling, zup, zdown, twin)

    loads = [
        pltpu.make_async_copy(src, dst, local.at[i])
        for i, (src, dst) in enumerate(
            [
                (lat_hbm, lat_in), (idx_hbm, idx_in), (iq_hbm, iq_in), (gain_hbm, gain_in),
                (seg_hbm, seg_in), (order_hbm, order_in), (mq_hbm, mraw),
            ]
        )
    ]
    for load in loads:
        load.start()
    barrier = pltpu.get_barrier_semaphore()
    for dev in near:
        pl.semaphore_signal(barrier, inc=1, device_id=dev, device_id_type=MESH)

    own = ctx_of(xl, y, core)
    loads[0].wait()
    loads[1].wait()
    keys = jnp.transpose(lat_in[...])
    lat[own, :, 0:LAT] = keys[0:HALF, 0:LAT]
    lat[own, :, LAT:2 * LAT] = keys[HALF:, 0:LAT]
    lat[own, :, 2 * LAT:] = jnp.concatenate([keys[0:HALF, LAT:], keys[HALF:, LAT:]], axis=1)
    for h in (0, 1):
        idx[own * 2 + h] = idx_in[h * HALF:(h + 1) * HALF, :]

    pl.semaphore_wait(barrier, len(near))

    started = []
    lanes = [0]

    def piece(b, c, h):
        if b == 0:
            return idx.at[c * 2 + h], rcv.at[c * 2 + h]
        return lat.at[c, pl.ds(h * (HALF // 2), HALF // 2)], lrcv.at[c * 2 + h]

    def send(b, c, h, dev):
        ref, sem = piece(b, c, h)
        copy = pltpu.make_async_remote_copy(
            src_ref=ref, dst_ref=ref, send_sem=snd.at[lanes[0]], recv_sem=sem,
            device_id=dev, device_id_type=MESH,
        )
        lanes[0] += 1
        copy.start()
        started.append(copy)

    def arrived(b, c, h):
        ref, sem = piece(b, c, h)
        pltpu.make_async_remote_copy(
            src_ref=ref, dst_ref=ref, send_sem=snd.at[0], recv_sem=sem,
            device_id=sibling, device_id_type=MESH,
        ).wait_recv()

    def goes(dist, h, way):
        return dist < far or (dist == far and h == way)

    def visits(s):
        for h in (0, 1):
            for way in (0, 1):
                if s == 0 and way == 1:
                    continue
                if s > 0 and not goes(s, h, way):
                    continue
                yield h, way, (y + ny - s) % ny if way == 0 else (y + s) % ny

    def ring_step(b, s):
        for h, way, yy in visits(s):
            c = ctx_of(xl, yy, core)
            if s > 0:
                arrived(b, c, h)
            for w in ((0, 1) if s == 0 else (way,)):
                if goes(s + 1, h, w):
                    send(b, c, h, up if w == 0 else down)
            send(b, c, h, cross[h])
            send(b, c, h, sibling)

    def cross_step(b, s):
        for h, way, yy in visits(s):
            c = ctx_of(1 - xl, yy, core)
            arrived(b, c, h)
            send(b, c, h, sibling)

    def sibling_wait(b):
        for xx in (0, 1):
            for yy in range(ny):
                for h in (0, 1):
                    arrived(b, ctx_of(xx, yy, 1 - core), h)

    def token_signal():
        pl.semaphore_signal(token.at[0], inc=1, device_id=zup, device_id_type=MESH)
        pl.semaphore_signal(token.at[1], inc=1, device_id=zdown, device_id_type=MESH)

    def token_wait():
        pl.semaphore_wait(token.at[0], 1)
        pl.semaphore_wait(token.at[1], 1)

    def exchange(kind, src, dst, i, start):
        to = (me_h + i) % nh
        frm = (me_h + nh - i) % nh
        copy = pltpu.make_async_remote_copy(
            src_ref=src(to), dst_ref=dst.at[me_h] if start else dst.at[frm],
            send_sem=xsend.at[kind, to],
            recv_sem=xrecv.at[kind, me_h] if start else xrecv.at[kind, frm],
            device_id=(me_c, to), device_id_type=MESH,
        )
        if start:
            copy.start()
        else:
            copy.wait()
        return 0

    def prepare_small():
        for load in loads[2:6]:
            load.wait()
        gains = jnp.concatenate(
            [gain_in[...].astype(F32), jnp.zeros((128 - iheads, 128), F32)], axis=0
        )
        gains = jnp.transpose(gains).astype(BF16)
        for i in range(8):
            rows = slice(16 * i, 16 * i + 16)
            iq_send[i, :, 0:iheads * 128] = iq_in[rows, :]
            iq_send[i, :, iheads * 128:] = gains[rows, :]
        order = order_in[...]
        blocks = order.shape[1]
        lane = lax.broadcasted_iota(jnp.int32, (1, blocks), 1)
        segs = seg_in[...].astype(F32)
        seg_row = lax.broadcasted_iota(jnp.int32, segs.shape, 0).astype(F32)
        counts = [total_of(jnp.where(segs == float(v), 1.0, 0.0)) for v in range(7)]
        for qb in (0, 1):
            mine_i = jnp.sum(jnp.where(lane == 2 * me_c + qb, order, 0), axis=1, keepdims=True)
            j = lax.broadcasted_iota(jnp.int32, (PAD_J, blocks), 0)
            want = jnp.maximum(mine_i - (reach - 1) + j, 0)
            at = lax.broadcasted_iota(jnp.int32, (PAD_J, blocks), 1)
            slot = jnp.sum(jnp.where(order == want, at, 0), axis=1, keepdims=True)
            slot = jnp.minimum(slot, blocks - 1)
            slot = jnp.broadcast_to(slot, (PAD_J, 128))
            slot_v[0, qb * PAD_J:(qb + 1) * PAD_J, :] = slot
            slot_v[1, qb * PAD_J:(qb + 1) * PAD_J, :] = slot >> 1
            slot_v[2, qb * PAD_J:(qb + 1) * PAD_J, :] = slot & 1
            mine = mine_i.astype(F32)
            first = mine - float(reach - 1)
            pair = jnp.floor(mine * 0.5)
            row = jnp.sum(jnp.where(seg_row == pair, segs, 0.0), axis=0, keepdims=True)
            row = jnp.where(mine - 2.0 * pair > 0.5, pltpu.roll(row, HALF, 1), row)
            sub = lax.broadcasted_iota(jnp.int32, (HALF, 128), 0)
            lan = lax.broadcasted_iota(jnp.int32, (HALF, 128), 1)
            seg_q = jnp.sum(jnp.where(sub == lan, row, 0.0), axis=1, keepdims=True)
            start = jnp.zeros((HALF, 1), F32)
            for v in range(7):
                start = start + jnp.where(seg_q > float(v), counts[v], 0.0)
            pos = mine * float(HALF) + lax.broadcasted_iota(
                jnp.int32, (HALF, 1), 0
            ).astype(F32)
            at = lax.broadcasted_iota(jnp.int32, (HALF, width), 1)
            row_at = lax.broadcasted_iota(jnp.int32, (HALF, width), 0)
            at = at + jnp.where((at < HALF) & (at <= row_at), width, 0)
            kp = first * float(HALF) + at.astype(F32)
            bias[qb] = jnp.where((kp >= start) & (kp <= pos), 0.0, FILL)
        copy = pltpu.make_async_copy(slot_v, slot_s, local.at[7])
        copy.start()
        copy.wait()

    def prepare_queries():
        loads[6].wait()
        for qb in (0, 1):
            for slab in range(4):
                rows = slice(qb * HALF + slab * 16, qb * HALF + slab * 16 + 16)
                for h in range(heads):
                    x = mraw[rows, h * kdim:(h + 1) * kdim]
                    at = slab * 16 * heads + h * 16
                    mq[qb, at:at + 16, 0:LAT] = x[:, 0:LAT]
                    mq[qb, at:at + 16, LAT:] = jnp.concatenate([x[:, LAT:], x[:, LAT:]], axis=1)

    def index_queries():
        def body(i, _):
            exchange(0, lambda to: iq_send.at[to // 2], iq_recv, i, False)
            return 0
        lax.fori_loop(1, nh, body, 0)
        iq_recv[me_h] = iq_send[me_h // 2]
        odd = me_h % 2

        def pick(s, _):
            x = iq_recv[s].astype(F32)
            x = jnp.where(odd == 0, x[0:8], x[8:16])
            at = pl.multiple_of(s * iheads * 8, 16)
            ilhs[pl.ds(at, iheads * 8), :] = jnp.concatenate(
                [x[:, k * 128:(k + 1) * 128] for k in range(iheads)], axis=0
            ).astype(BF16)
            g = x[:, iheads * 128:]
            iwide[pl.ds(at, iheads * 8), :] = jnp.concatenate(
                [jnp.broadcast_to(g[:, k:k + 1], (8, 128)) for k in range(iheads)], axis=0
            )
            return 0

        lax.fori_loop(0, nh, pick, 0)

    mine_qb = me_h // half_h
    mine_row = (me_h % half_h) * 8

    def index_scores():
        rows = ilhs.shape[0]

        def scores(first, count, at):
            ks = [idx[slot_s[0, mine_qb * PAD_J + first + k, 0]] for k in range(count)]
            ks += ks[-1:] * (-count % 2)
            dots = dot_nt(ilhs[...], jnp.concatenate(ks, axis=0))
            for k in range(dots.shape[1] // 128):
                part = jnp.maximum(dots[:, k * 128:(k + 1) * 128], 0.0) * iwide[...]
                part = jnp.sum(part.reshape(rows // 8, 8, 128), axis=0)
                lo = at + k * 128
                if lo < fold:
                    ipack[0:8, lo:lo + 128] = part
                else:
                    ipack[8:16, lo - fold:lo - fold + 128] = part

        for first in range(0, reach - 1, GROUP):
            scores(first, GROUP, first * HALF)
        last = ipack[0:8, 0:128]
        scores(reach - 1, 1, 0)
        lane = lax.broadcasted_iota(jnp.int32, (8, 128), 1)
        row = mine_row + lax.broadcasted_iota(jnp.int32, (8, 128), 0)
        ipack[0:8, 0:128] = jnp.where((lane < HALF) & (lane <= row), ipack[0:8, 0:128], last)

    def packed(x):
        return jnp.concatenate([x[:, 0:fold], x[:, fold:]], axis=0)

    def packed_bias():
        return packed(bias[mine_qb, pl.ds(pl.multiple_of(mine_row, 8), 8), :])

    def both(x, op):
        return op(x[0:8], x[8:16])

    def key_block(qb, j):
        rows = lat[slot_s[1, qb * PAD_J + j, 0]]
        odd = slot_s[2, qb * PAD_J + j, 0]
        lane = lax.broadcasted_iota(jnp.int32, (HALF, 128), 1)
        second = lane * 0 + odd > 0
        second = jnp.concatenate([second] * (LAT // 128), axis=1)
        main = jnp.where(second, rows[:, LAT:2 * LAT], rows[:, 0:LAT])
        tail = rows[:, 2 * LAT:]
        tail = jnp.where(lane // HALF == odd, tail, jnp.zeros_like(tail))
        return jnp.concatenate([main, tail], axis=1)

    def scores_of(qb):
        def body(g, _):
            ks = jnp.concatenate([key_block(qb, g * GROUP + k) for k in range(GROUP)], axis=0)
            at = pl.ds(pl.multiple_of(g * GROUP * HALF, 256), GROUP * HALF)
            score[:, at] = dot_nt(mq[qb], ks)
            return 0

        lax.fori_loop(0, (reach - 1) // GROUP, body, 0)
        last = key_block(qb, reach - 1)
        s = dot_nt(mq[qb], jnp.concatenate([last, last], axis=0))
        at = lax.broadcasted_iota(jnp.int32, s.shape, 0)
        row = at // (16 * heads) * 16 + at % 16
        lane = lax.broadcasted_iota(jnp.int32, s.shape, 1)
        score[:, 0:128] = jnp.where((lane < HALF) & (lane <= row), s, score[:, 0:128])

    def shares_of(qb):
        def body(i, _):
            g = (me_h + i) % half_h
            d = qb * half_h + g
            b = bias[qb, pl.ds(pl.multiple_of(g * 8, 8), 8), :]
            base = (g // 2) * (16 * heads) + (g % 2) * 8
            acc = jnp.zeros((8, width), F32)
            for h in range(heads):
                s = score[pl.ds(pl.multiple_of(base + h * 16, 8), 8), :] + b
                top = jnp.max(s, axis=1, keepdims=True)
                p = jnp.exp2((s - top) * EXP_SCALE)
                acc = acc + p * (1.0 / jnp.sum(p, axis=1, keepdims=True))
            share = packed(acc)
            tsend[d] = share.astype(BF16)

            @pl.when(d == me_h)
            def _():
                town[...] = share

            @pl.when(d != me_h)
            def _():
                pltpu.make_async_remote_copy(
                    src_ref=tsend.at[d], dst_ref=trecv.at[me_h],
                    send_sem=xsend.at[1, d], recv_sem=xrecv.at[1, me_h],
                    device_id=(me_c, d), device_id_type=MESH,
                ).start()

            return 0

        lax.fori_loop(1, half_h + 1, body, 0)

    ring_step(0, 0)
    ring_step(1, 0)
    token_signal()
    prepare_small()
    rounds = nz // 2
    token_wait()
    done = 1
    if done < rounds:
        token_signal()
    prepare_queries()

    def token_round():
        token_wait()
        done_rounds[0] += 1
        if done_rounds[0] < rounds:
            token_signal()

    done_rounds = [done]
    steps = [(0, s) for s in range(1, far + 1)]
    for s in range(1, far):
        steps.insert(min(3 * s - 1, len(steps)), (1, s))
    for n, (b, s) in enumerate(steps):
        ring_step(b, s)
        cross_step(b, s - 1)
        if n == len(steps) - 2:
            cross_step(0, far)
        if done_rounds[0] < rounds:
            token_round()
            if done_rounds[0] == rounds:
                lax.fori_loop(
                    1, nh,
                    lambda i, _: exchange(0, lambda to: iq_send.at[to // 2], iq_recv, i, True), 0,
                )
    index_queries()
    sibling_wait(0)
    index_scores()
    ring_step(1, far)
    cross_step(1, far - 1)
    cross_step(1, far)
    seen_bias = packed_bias()
    index_score = ipack[...]
    masked = index_score + seen_bias
    top = both(jnp.max(masked, axis=1, keepdims=True), jnp.maximum)
    tops = jnp.concatenate([top, top], axis=0)
    exp_sum = both(jnp.sum(jnp.exp(masked - tops), axis=1, keepdims=True), jnp.add)
    lse = top + jnp.log(exp_sum)
    sibling_wait(1)

    for qb in (0, 1):
        scores_of(qb)
        shares_of(qb)

    def add_share(i, acc):
        exchange(1, lambda to: tsend.at[to], trecv, i, False)
        return acc + trecv[(me_h + nh - i) % nh].astype(F32)

    target = lax.fori_loop(1, nh, add_share, town[...]) * (1.0 / HEADS)
    positive = target > 0.0
    logs = jnp.log(jnp.where(positive, target, 1.0))
    gain = both(
        jnp.sum(target * (logs - index_score), axis=1, keepdims=True), jnp.add
    )
    mass = both(jnp.sum(target, axis=1, keepdims=True), jnp.add)
    kl = gain + lse * mass + (1.0 - mass)
    sub = lax.broadcasted_iota(jnp.int32, (8, 128), 0)
    lan = lax.broadcasted_iota(jnp.int32, (8, 128), 1)
    mine = jnp.where(lan == 8 * me_h + sub, kl, 0.0)
    fsend[...] = mine
    lax.fori_loop(1, nh, lambda i, _: exchange(2, lambda to: fsend, frecv, i, True), 0)
    frecv[me_h] = mine
    for copy in started:
        copy.wait_send()
    lax.fori_loop(1, nh, lambda i, _: exchange(2, lambda to: fsend, frecv, i, False), 0)
    out_ref[...] = jnp.sum(jnp.sum(frecv[...], axis=0), axis=0, keepdims=True)


def per_device(
    latent_keys, index_keys, main_query, index_query, index_weight, segment_ids, block_order
):
    rows, kdim = latent_keys.shape
    nc, nh = lax.axis_size("ctx"), lax.axis_size("head")
    ny = nc // 4
    blocks = 2 * nc
    reach = nc // 2 + 1
    heads = main_query.shape[1] // kdim
    iheads = index_weight.shape[1]
    width = (reach - 1) * HALF
    fold = width // 2
    wide = heads * HALF
    vmem = pl.BlockSpec(memory_space=pltpu.VMEM)
    hbm = pl.BlockSpec(memory_space=pl.ANY)
    dma = pltpu.SemaphoreType.DMA
    out = pl.pallas_call(
        functools.partial(fused, ny, nh, reach, heads, iheads),
        out_shape=jax.ShapeDtypeStruct((1, rows), F32),
        in_specs=[hbm] * 7,
        out_specs=vmem,
        scratch_shapes=[
            pltpu.VMEM((kdim, rows), BF16),
            pltpu.VMEM((rows, 128), BF16),
            pltpu.VMEM((rows, iheads * 128), BF16),
            pltpu.VMEM((iheads, rows), BF16),
            pltpu.VMEM((blocks * HALF // 128, 128), jnp.int32),
            pltpu.VMEM((1, blocks), jnp.int32),
            pltpu.VMEM((nc, HALF, 2 * kdim), BF16),
            pltpu.VMEM((blocks, HALF, 128), BF16),
            pltpu.VMEM((rows, heads * kdim), BF16),
            pltpu.VMEM((2, wide, LAT + 2 * ROPE), BF16),
            pltpu.VMEM((wide, width), F32),
            pltpu.VMEM((2, HALF, width), F32),
            pltpu.VMEM((8, 16, iheads * 128 + 128), BF16),
            pltpu.VMEM((nh, 16, iheads * 128 + 128), BF16),
            pltpu.VMEM((nh * iheads * 8, 128), BF16),
            pltpu.VMEM((nh * iheads * 8, 128), F32),
            pltpu.VMEM((16, fold), F32),
            pltpu.VMEM((3, 2 * PAD_J, 128), jnp.int32),
            pltpu.SMEM((3, 2 * PAD_J, 128), jnp.int32),
            pltpu.VMEM((nh, 16, fold), BF16),
            pltpu.VMEM((nh, 16, fold), BF16),
            pltpu.VMEM((16, fold), F32),
            pltpu.VMEM((8, 128), F32),
            pltpu.VMEM((nh, 8, 128), F32),
            dma((4 * (7 * ny + 4),)),
            dma((blocks,)),
            dma((blocks,)),
            dma((3, nh)),
            dma((3, nh)),
            dma((8,)),
            pltpu.SemaphoreType.REGULAR((2,)),
        ],
        compiler_params=pltpu.CompilerParams(
            collective_id=0, has_side_effects=True, vmem_limit_bytes=60 * 2**20
        ),
    )(
        latent_keys.T, index_keys, main_query, index_query, index_weight.T,
        segment_ids.reshape(-1, 128), block_order.reshape(1, blocks),
    )
    return out.reshape(rows)


def solution(mesh):
    in_specs = (
        P("ctx", None),
        P("ctx", None),
        P("ctx", "head"),
        P("ctx", "head"),
        P("ctx", "head"),
        P(),
        P(),
    )
    return jax.shard_map(
        per_device, mesh=mesh, in_specs=in_specs, out_specs=P("ctx"), check_vma=False
    )
```

```python
import functools
import math

import jax
import jax.numpy as jnp
from jax import lax
from jax.experimental import pallas as pl
from jax.experimental.pallas import tpu as pltpu
from jax.sharding import PartitionSpec as P

HEADS = 128
HALF = 64
LAT = 512
ROPE = 64
FILL = -1e30
EXP_SCALE = 192.0 ** (-0.5) * math.log2(math.e)
MESH = pl.DeviceIdType.MESH
NT = (((1,), (1,)), ((), ()))
F32 = jnp.float32
BF16 = jnp.bfloat16
GROUP = 4
PAD_J = 24


def dot_nt(a, b):
    return lax.dot_general(a, b, NT, preferred_element_type=F32)


def total_of(x):
    return jnp.sum(jnp.sum(x, axis=1, keepdims=True), axis=0, keepdims=True)


def fused(
    ny, nh, reach, heads, iheads,
    lat_hbm, idx_hbm, mq_hbm, iq_hbm, gain_hbm, seg_hbm, order_hbm,
    out_ref,
    lat_in, idx_in, iq_in, gain_in, seg_in, order_in,
    lat, mraw, mq, score, bias, iq_send, iq_recv, ilhs, iwide, ipack,
    slot_v, slot_s, tsend, trecv, town, fsend, frecv,
    snd, rcv, xsend, xrecv, local, token,
):
    kdim = LAT + ROPE
    me_c, me_h = lax.axis_index("ctx"), lax.axis_index("head")
    core = me_c % 2
    y = (me_c // 2) % ny
    xl = me_c // (2 * ny)
    xh = me_h % 2
    z = me_h // 2
    nz = nh // 2
    far = ny // 2
    half_h = nh // 2
    width = (reach - 1) * HALF
    fold = width // 2

    def ctx_of(xl_, y_, core_):
        return (xl_ * ny + y_) * 2 + core_

    up = (ctx_of(xl, (y + 1) % ny, core), me_h)
    down = (ctx_of(xl, (y + ny - 1) % ny, core), me_h)
    cross = (
        (ctx_of(1 - xl, y, core), me_h),
        (ctx_of(1 - xl, y, core), z * 2 + 1 - xh),
    )
    sibling = (ctx_of(xl, y, 1 - core), me_h)
    zup = (me_c, ((z + 1) % nz) * 2 + xh)
    zdown = (me_c, ((z + nz - 1) % nz) * 2 + xh)
    twin = (me_c, z * 2 + 1 - xh)
    near = (up, down, cross[0], cross[1], sibling, zup, zdown, twin)

    loads = [
        pltpu.make_async_copy(src, dst, local.at[i])
        for i, (src, dst) in enumerate(
            [
                (lat_hbm, lat_in), (idx_hbm, idx_in), (iq_hbm, iq_in), (gain_hbm, gain_in),
                (seg_hbm, seg_in), (order_hbm, order_in), (mq_hbm, mraw),
            ]
        )
    ]
    for load in loads:
        load.start()
    barrier = pltpu.get_barrier_semaphore()
    for dev in near:
        pl.semaphore_signal(barrier, inc=1, device_id=dev, device_id_type=MESH)

    own = ctx_of(xl, y, core)
    loads[0].wait()
    loads[1].wait()
    keys = jnp.transpose(lat_in[...])
    lat[own, :, 0:LAT] = keys[0:HALF, 0:LAT]
    lat[own, :, LAT:2 * LAT] = keys[HALF:, 0:LAT]
    lat[own, :, 2 * LAT:2 * kdim] = jnp.concatenate([keys[0:HALF, LAT:], keys[HALF:, LAT:]], axis=1)
    for h in (0, 1):
        at = 2 * kdim + h * 128
        lat[own, :, at:at + 128] = idx_in[h * HALF:(h + 1) * HALF, :]

    pl.semaphore_wait(barrier, len(near))

    started = []

    def piece(c, h):
        return lat.at[c, pl.ds(h * (HALF // 2), HALF // 2)], rcv.at[c * 2 + h]

    def send(c, h, dev):
        ref, sem = piece(c, h)
        copy = pltpu.make_async_remote_copy(
            src_ref=ref, dst_ref=ref, send_sem=snd.at[len(started)], recv_sem=sem,
            device_id=dev, device_id_type=MESH,
        )
        copy.start()
        started.append(copy)

    def arrived(c, h):
        ref, sem = piece(c, h)
        pltpu.make_async_remote_copy(
            src_ref=ref, dst_ref=ref, send_sem=snd.at[0], recv_sem=sem,
            device_id=sibling, device_id_type=MESH,
        ).wait_recv()

    def goes(dist, h, way):
        return dist < far or (dist == far and h == way)

    def visits(s):
        for h in (0, 1):
            for way in (0, 1):
                if s == 0 and way == 1:
                    continue
                if s > 0 and not goes(s, h, way):
                    continue
                yield h, way, (y + ny - s) % ny if way == 0 else (y + s) % ny

    def ring_step(s):
        for h, way, yy in visits(s):
            c = ctx_of(xl, yy, core)
            if s > 0:
                arrived(c, h)
            for w in ((0, 1) if s == 0 else (way,)):
                if goes(s + 1, h, w):
                    send(c, h, up if w == 0 else down)
            send(c, h, cross[h])
            send(c, h, sibling)

    def cross_step(s):
        for h, way, yy in visits(s):
            c = ctx_of(1 - xl, yy, core)
            arrived(c, h)
            send(c, h, sibling)

    def sibling_wait():
        for xx in (0, 1):
            for yy in range(ny):
                for h in (0, 1):
                    arrived(ctx_of(xx, yy, 1 - core), h)

    def token_signal():
        pl.semaphore_signal(token.at[0], inc=1, device_id=zup, device_id_type=MESH)
        pl.semaphore_signal(token.at[1], inc=1, device_id=zdown, device_id_type=MESH)

    def token_wait():
        pl.semaphore_wait(token.at[0], 1)
        pl.semaphore_wait(token.at[1], 1)

    def exchange(kind, src, dst, k, start):
        i = half_h + (k // 2) * (2 * (k % 2) - 1)
        to = (me_h + i) % nh
        frm = (me_h + nh - i) % nh
        copy = pltpu.make_async_remote_copy(
            src_ref=src(to), dst_ref=dst.at[me_h] if start else dst.at[frm],
            send_sem=xsend.at[kind, to],
            recv_sem=xrecv.at[kind, me_h] if start else xrecv.at[kind, frm],
            device_id=(me_c, to), device_id_type=MESH,
        )
        if start:
            copy.start()
        else:
            copy.wait()
        return 0

    def prepare_small():
        for load in loads[2:6]:
            load.wait()
        gains = jnp.concatenate(
            [gain_in[...].astype(F32), jnp.zeros((128 - iheads, 128), F32)], axis=0
        )
        gains = jnp.transpose(gains).astype(BF16)
        for i in range(8):
            rows = slice(16 * i, 16 * i + 16)
            iq_send[i, :, 0:iheads * 128] = iq_in[rows, :]
            iq_send[i, :, iheads * 128:] = gains[rows, :]
        order = order_in[...]
        blocks = order.shape[1]
        lane = lax.broadcasted_iota(jnp.int32, (1, blocks), 1)
        segs = seg_in[...].astype(F32)
        seg_row = lax.broadcasted_iota(jnp.int32, segs.shape, 0).astype(F32)
        counts = [total_of(jnp.where(segs == float(v), 1.0, 0.0)) for v in range(7)]
        for qb in (0, 1):
            mine_i = jnp.sum(jnp.where(lane == 2 * me_c + qb, order, 0), axis=1, keepdims=True)
            j = lax.broadcasted_iota(jnp.int32, (PAD_J, blocks), 0)
            want = jnp.maximum(mine_i - (reach - 1) + j, 0)
            at = lax.broadcasted_iota(jnp.int32, (PAD_J, blocks), 1)
            slot = jnp.sum(jnp.where(order == want, at, 0), axis=1, keepdims=True)
            slot = jnp.minimum(slot, blocks - 1)
            slot = jnp.broadcast_to(slot, (PAD_J, 128))
            slot_v[0, qb * PAD_J:(qb + 1) * PAD_J, :] = slot
            slot_v[1, qb * PAD_J:(qb + 1) * PAD_J, :] = slot >> 1
            slot_v[2, qb * PAD_J:(qb + 1) * PAD_J, :] = slot & 1
            mine = mine_i.astype(F32)
            first = mine - float(reach - 1)
            pair = jnp.floor(mine * 0.5)
            row = jnp.sum(jnp.where(seg_row == pair, segs, 0.0), axis=0, keepdims=True)
            row = jnp.where(mine - 2.0 * pair > 0.5, pltpu.roll(row, HALF, 1), row)
            sub = lax.broadcasted_iota(jnp.int32, (HALF, 128), 0)
            lan = lax.broadcasted_iota(jnp.int32, (HALF, 128), 1)
            seg_q = jnp.sum(jnp.where(sub == lan, row, 0.0), axis=1, keepdims=True)
            start = jnp.zeros((HALF, 1), F32)
            for v in range(7):
                start = start + jnp.where(seg_q > float(v), counts[v], 0.0)
            pos = mine * float(HALF) + lax.broadcasted_iota(
                jnp.int32, (HALF, 1), 0
            ).astype(F32)
            at = lax.broadcasted_iota(jnp.int32, (HALF, width), 1)
            row_at = lax.broadcasted_iota(jnp.int32, (HALF, width), 0)
            at = at + jnp.where((at < HALF) & (at <= row_at), width, 0)
            kp = first * float(HALF) + at.astype(F32)
            bias[qb] = jnp.where((kp >= start) & (kp <= pos), 0.0, FILL)
        copy = pltpu.make_async_copy(slot_v, slot_s, local.at[7])
        copy.start()
        copy.wait()

    def prepare_queries():
        loads[6].wait()
        for qb in (0, 1):
            for slab in range(4):
                rows = slice(qb * HALF + slab * 16, qb * HALF + slab * 16 + 16)
                for h in range(heads):
                    x = mraw[rows, h * kdim:(h + 1) * kdim]
                    at = slab * 16 * heads + h * 16
                    mq[qb, at:at + 16, 0:LAT] = x[:, 0:LAT]
                    mq[qb, at:at + 16, LAT:] = jnp.concatenate([x[:, LAT:], x[:, LAT:]], axis=1)

    def index_queries():
        def body(i, _):
            exchange(0, lambda to: iq_send.at[to // 2], iq_recv, i, False)
            return 0
        lax.fori_loop(1, nh, body, 0)
        iq_recv[me_h] = iq_send[me_h // 2]
        odd = me_h % 2

        def pick(s, _):
            x = iq_recv[s].astype(F32)
            x = jnp.where(odd == 0, x[0:8], x[8:16])
            at = pl.multiple_of(s * iheads * 8, 16)
            ilhs[pl.ds(at, iheads * 8), :] = jnp.concatenate(
                [x[:, k * 128:(k + 1) * 128] for k in range(iheads)], axis=0
            ).astype(BF16)
            g = x[:, iheads * 128:]
            iwide[pl.ds(at, iheads * 8), :] = jnp.concatenate(
                [jnp.broadcast_to(g[:, k:k + 1], (8, 128)) for k in range(iheads)], axis=0
            )
            return 0

        lax.fori_loop(0, nh, pick, 0)

    mine_qb = me_h // half_h
    mine_row = (me_h % half_h) * 8

    def index_scores():
        rows = ilhs.shape[0]

        def block(j):
            rows = lat[slot_s[1, mine_qb * PAD_J + j, 0]]
            odd = slot_s[2, mine_qb * PAD_J + j, 0]
            lane = lax.broadcasted_iota(jnp.int32, (HALF, 128), 1)
            return jnp.where(
                lane * 0 + odd > 0, rows[:, 2 * kdim + 128:], rows[:, 2 * kdim:2 * kdim + 128]
            )

        def scores(first, count, at):
            ks = [block(first + k) for k in range(count)]
            ks += ks[-1:] * (-count % 2)
            dots = dot_nt(ilhs[...], jnp.concatenate(ks, axis=0))
            for k in range(dots.shape[1] // 128):
                part = jnp.maximum(dots[:, k * 128:(k + 1) * 128], 0.0) * iwide[...]
                part = jnp.sum(part.reshape(rows // 8, 8, 128), axis=0)
                lo = at + k * 128
                if lo < fold:
                    ipack[0:8, lo:lo + 128] = part
                else:
                    ipack[8:16, lo - fold:lo - fold + 128] = part

        for first in range(0, reach - 1, GROUP):
            scores(first, GROUP, first * HALF)
        last = ipack[0:8, 0:128]
        scores(reach - 1, 1, 0)
        lane = lax.broadcasted_iota(jnp.int32, (8, 128), 1)
        row = mine_row + lax.broadcasted_iota(jnp.int32, (8, 128), 0)
        ipack[0:8, 0:128] = jnp.where((lane < HALF) & (lane <= row), ipack[0:8, 0:128], last)

    def packed(x):
        return jnp.concatenate([x[:, 0:fold], x[:, fold:]], axis=0)

    def packed_bias():
        return packed(bias[mine_qb, pl.ds(pl.multiple_of(mine_row, 8), 8), :])

    def both(x, op):
        return op(x[0:8], x[8:16])

    def key_block(qb, j):
        rows = lat[slot_s[1, qb * PAD_J + j, 0]]
        odd = slot_s[2, qb * PAD_J + j, 0]
        lane = lax.broadcasted_iota(jnp.int32, (HALF, 128), 1)
        second = lane * 0 + odd > 0
        second = jnp.concatenate([second] * (LAT // 128), axis=1)
        main = jnp.where(second, rows[:, LAT:2 * LAT], rows[:, 0:LAT])
        tail = rows[:, 2 * LAT:2 * kdim]
        tail = jnp.where(lane // HALF == odd, tail, jnp.zeros_like(tail))
        return jnp.concatenate([main, tail], axis=1)

    def scores_of(qb):
        def body(g, _):
            ks = jnp.concatenate([key_block(qb, g * GROUP + k) for k in range(GROUP)], axis=0)
            at = pl.ds(pl.multiple_of(g * GROUP * HALF, 256), GROUP * HALF)
            score[:, at] = dot_nt(mq[qb], ks)
            return 0

        lax.fori_loop(0, (reach - 1) // GROUP, body, 0)
        last = key_block(qb, reach - 1)
        s = dot_nt(mq[qb], jnp.concatenate([last, last], axis=0))
        at = lax.broadcasted_iota(jnp.int32, s.shape, 0)
        row = at // (16 * heads) * 16 + at % 16
        lane = lax.broadcasted_iota(jnp.int32, s.shape, 1)
        score[:, 0:128] = jnp.where((lane < HALF) & (lane <= row), s, score[:, 0:128])

    def shares_of(qb):
        def body(i, _):
            g = (me_h + i) % half_h
            d = qb * half_h + g
            b = bias[qb, pl.ds(pl.multiple_of(g * 8, 8), 8), :]
            base = (g // 2) * (16 * heads) + (g % 2) * 8
            acc = jnp.zeros((8, width), F32)
            for h in range(heads):
                s = score[pl.ds(pl.multiple_of(base + h * 16, 8), 8), :] + b
                top = jnp.max(s, axis=1, keepdims=True)
                p = jnp.exp2((s - top) * EXP_SCALE)
                acc = acc + p * (1.0 / jnp.sum(p, axis=1, keepdims=True))
            share = packed(acc)
            tsend[d] = share.astype(BF16)

            @pl.when(d == me_h)
            def _():
                town[...] = share

            @pl.when(d != me_h)
            def _():
                pltpu.make_async_remote_copy(
                    src_ref=tsend.at[d], dst_ref=trecv.at[me_h],
                    send_sem=xsend.at[1, d], recv_sem=xrecv.at[1, me_h],
                    device_id=(me_c, d), device_id_type=MESH,
                ).start()

            return 0

        lax.fori_loop(1, half_h + 1, body, 0, unroll=2)

    ring_step(0)
    token_signal()
    prepare_small()
    rounds = nz // 2
    token_wait()
    done = 1
    if done < rounds:
        token_signal()
    prepare_queries()
    for s in range(1, far + 1):
        ring_step(s)
        for _ in range(2):
            if done < rounds:
                token_wait()
                done += 1
                if done < rounds:
                    token_signal()
                else:
                    lax.fori_loop(
                        1, nh,
                        lambda i, _: exchange(0, lambda to: iq_send.at[to // 2], iq_recv, i, True),
                        0,
                    )
        cross_step(s - 1)
    cross_step(far)
    sibling_wait()

    for qb in (0, 1):
        scores_of(qb)
        shares_of(qb)

    index_queries()
    index_scores()
    seen_bias = packed_bias()
    index_score = ipack[...]
    masked = index_score + seen_bias
    top = both(jnp.max(masked, axis=1, keepdims=True), jnp.maximum)
    tops = jnp.concatenate([top, top], axis=0)
    exp_sum = both(jnp.sum(jnp.exp(masked - tops), axis=1, keepdims=True), jnp.add)
    lse = top + jnp.log(exp_sum)
    for copy in started:
        copy.wait_send()

    def add_share(i, acc):
        exchange(1, lambda to: tsend.at[to], trecv, i, False)
        return acc + trecv[(me_h + nh - (half_h + (i // 2) * (2 * (i % 2) - 1))) % nh].astype(F32)

    target = lax.fori_loop(1, nh, add_share, town[...]) * (1.0 / HEADS)
    positive = target > 0.0
    logs = jnp.log(jnp.where(positive, target, 1.0))
    gain = both(
        jnp.sum(target * (logs - index_score), axis=1, keepdims=True), jnp.add
    )
    mass = both(jnp.sum(target, axis=1, keepdims=True), jnp.add)
    kl = gain + lse * mass + (1.0 - mass)
    sub = lax.broadcasted_iota(jnp.int32, (8, 128), 0)
    lan = lax.broadcasted_iota(jnp.int32, (8, 128), 1)
    mine = jnp.where(lan == 8 * me_h + sub, kl, 0.0)
    fsend[...] = mine
    lax.fori_loop(1, nh, lambda i, _: exchange(2, lambda to: fsend, frecv, i, True), 0)
    frecv[me_h] = mine
    lax.fori_loop(1, nh, lambda i, _: exchange(2, lambda to: fsend, frecv, i, False), 0)
    out_ref[...] = jnp.sum(jnp.sum(frecv[...], axis=0), axis=0, keepdims=True)


def per_device(
    latent_keys, index_keys, main_query, index_query, index_weight, segment_ids, block_order
):
    rows, kdim = latent_keys.shape
    nc, nh = lax.axis_size("ctx"), lax.axis_size("head")
    ny = nc // 4
    blocks = 2 * nc
    reach = nc // 2 + 1
    heads = main_query.shape[1] // kdim
    iheads = index_weight.shape[1]
    width = (reach - 1) * HALF
    fold = width // 2
    wide = heads * HALF
    vmem = pl.BlockSpec(memory_space=pltpu.VMEM)
    hbm = pl.BlockSpec(memory_space=pl.ANY)
    dma = pltpu.SemaphoreType.DMA
    out = pl.pallas_call(
        functools.partial(fused, ny, nh, reach, heads, iheads),
        out_shape=jax.ShapeDtypeStruct((1, rows), F32),
        in_specs=[hbm] * 7,
        out_specs=vmem,
        scratch_shapes=[
            pltpu.VMEM((kdim, rows), BF16),
            pltpu.VMEM((rows, 128), BF16),
            pltpu.VMEM((rows, iheads * 128), BF16),
            pltpu.VMEM((iheads, rows), BF16),
            pltpu.VMEM((blocks * HALF // 128, 128), jnp.int32),
            pltpu.VMEM((1, blocks), jnp.int32),
            pltpu.VMEM((nc, HALF, 2 * kdim + 256), BF16),
            pltpu.VMEM((rows, heads * kdim), BF16),
            pltpu.VMEM((2, wide, LAT + 2 * ROPE), BF16),
            pltpu.VMEM((wide, width), F32),
            pltpu.VMEM((2, HALF, width), F32),
            pltpu.VMEM((8, 16, iheads * 128 + 128), BF16),
            pltpu.VMEM((nh, 16, iheads * 128 + 128), BF16),
            pltpu.VMEM((nh * iheads * 8, 128), BF16),
            pltpu.VMEM((nh * iheads * 8, 128), F32),
            pltpu.VMEM((16, fold), F32),
            pltpu.VMEM((3, 2 * PAD_J, 128), jnp.int32),
            pltpu.SMEM((3, 2 * PAD_J, 128), jnp.int32),
            pltpu.VMEM((nh, 16, fold), BF16),
            pltpu.VMEM((nh, 16, fold), BF16),
            pltpu.VMEM((16, fold), F32),
            pltpu.VMEM((8, 128), F32),
            pltpu.VMEM((nh, 8, 128), F32),
            dma((2 * (ny - 1) + 6 * ny,)),
            dma((blocks,)),
            dma((3, nh)),
            dma((3, nh)),
            dma((8,)),
            pltpu.SemaphoreType.REGULAR((2,)),
        ],
        compiler_params=pltpu.CompilerParams(
            collective_id=0, has_side_effects=True, vmem_limit_bytes=60 * 2**20
        ),
    )(
        latent_keys.T, index_keys, main_query, index_query, index_weight.T,
        segment_ids.reshape(-1, 128), block_order.reshape(1, blocks),
    )
    return out.reshape(rows)


def solution(mesh):
    in_specs = (
        P("ctx", None),
        P("ctx", None),
        P("ctx", "head"),
        P("ctx", "head"),
        P("ctx", "head"),
        P(),
        P(),
    )
    return jax.shard_map(
        per_device, mesh=mesh, in_specs=in_specs, out_specs=P("ctx"), check_vma=False
    )
```

```python
import functools
import math

import jax
import jax.numpy as jnp
from jax import lax
from jax.experimental import pallas as pl
from jax.experimental.pallas import tpu as pltpu
from jax.sharding import PartitionSpec as P

HEADS = 128
HALF = 64
LAT = 512
ROPE = 64
FILL = -1e30
EXP_SCALE = 192.0 ** (-0.5) * math.log2(math.e)
MESH = pl.DeviceIdType.MESH
NT = (((1,), (1,)), ((), ()))
F32 = jnp.float32
BF16 = jnp.bfloat16
GROUP = 4
UNROLL_M = 4
PAD_J = 24


def dot_nt(a, b):
    return lax.dot_general(a, b, NT, preferred_element_type=F32)


def total_of(x):
    return jnp.sum(jnp.sum(x, axis=1, keepdims=True), axis=0, keepdims=True)


def fused(
    ny, nh, reach, heads, iheads,
    lat_hbm, idx_hbm, mq_hbm, iq_hbm, gain_hbm, seg_hbm, order_hbm,
    out_ref,
    lat_in, idx_in, iq_in, gain_in, seg_in, order_in,
    lat, mraw, mq, score, bias, iq_send, iq_recv, ilhs, iwide, ipack,
    slot_v, slot_s, tsend, trecv, town, kept, fsend, frecv,
    snd, rcv, xsend, xrecv, local, token,
):
    kdim = LAT + ROPE
    me_c, me_h = lax.axis_index("ctx"), lax.axis_index("head")
    core = me_c % 2
    y = (me_c // 2) % ny
    xl = me_c // (2 * ny)
    xh = me_h % 2
    z = me_h // 2
    nz = nh // 2
    far = ny // 2
    half_h = nh // 2
    width = (reach - 1) * HALF
    fold = width // 2

    def ctx_of(xl_, y_, core_):
        return (xl_ * ny + y_) * 2 + core_

    up = (ctx_of(xl, (y + 1) % ny, core), me_h)
    down = (ctx_of(xl, (y + ny - 1) % ny, core), me_h)
    cross = (
        (ctx_of(1 - xl, y, core), me_h),
        (ctx_of(1 - xl, y, core), z * 2 + 1 - xh),
    )
    sibling = (ctx_of(xl, y, 1 - core), me_h)
    zup = (me_c, ((z + 1) % nz) * 2 + xh)
    zdown = (me_c, ((z + nz - 1) % nz) * 2 + xh)
    twin = (me_c, z * 2 + 1 - xh)
    near = (up, down, cross[0], cross[1], sibling, zup, zdown, twin)

    loads = [
        pltpu.make_async_copy(src, dst, local.at[i])
        for i, (src, dst) in enumerate(
            [
                (lat_hbm, lat_in), (idx_hbm, idx_in), (iq_hbm, iq_in), (gain_hbm, gain_in),
                (seg_hbm, seg_in), (order_hbm, order_in), (mq_hbm, mraw),
            ]
        )
    ]
    for load in loads:
        load.start()
    barrier = pltpu.get_barrier_semaphore()
    for dev in near:
        pl.semaphore_signal(barrier, inc=1, device_id=dev, device_id_type=MESH)

    own = ctx_of(xl, y, core)
    loads[0].wait()
    loads[1].wait()
    keys = jnp.transpose(lat_in[...])
    lat[own, :, 0:LAT] = keys[0:HALF, 0:LAT]
    lat[own, :, LAT:2 * LAT] = keys[HALF:, 0:LAT]
    lat[own, :, 2 * LAT:2 * kdim] = jnp.concatenate([keys[0:HALF, LAT:], keys[HALF:, LAT:]], axis=1)
    for h in (0, 1):
        at = 2 * kdim + h * 128
        lat[own, :, at:at + 128] = idx_in[h * HALF:(h + 1) * HALF, :]

    pl.semaphore_wait(barrier, len(near))

    started = []

    def piece(c, h):
        return lat.at[c, pl.ds(h * (HALF // 2), HALF // 2)], rcv.at[c * 2 + h]

    def send(c, h, dev):
        ref, sem = piece(c, h)
        copy = pltpu.make_async_remote_copy(
            src_ref=ref, dst_ref=ref, send_sem=snd.at[len(started)], recv_sem=sem,
            device_id=dev, device_id_type=MESH,
        )
        copy.start()
        started.append(copy)

    def arrived(c, h):
        ref, sem = piece(c, h)
        pltpu.make_async_remote_copy(
            src_ref=ref, dst_ref=ref, send_sem=snd.at[0], recv_sem=sem,
            device_id=sibling, device_id_type=MESH,
        ).wait_recv()

    def goes(dist, h, way):
        return dist < far or (dist == far and h == way)

    def visits(s):
        for h in (0, 1):
            for way in (0, 1):
                if s == 0 and way == 1:
                    continue
                if s > 0 and not goes(s, h, way):
                    continue
                yield h, way, (y + ny - s) % ny if way == 0 else (y + s) % ny

    def ring_step(s):
        for h, way, yy in visits(s):
            c = ctx_of(xl, yy, core)
            if s > 0:
                arrived(c, h)
            for w in ((0, 1) if s == 0 else (way,)):
                if goes(s + 1, h, w):
                    send(c, h, up if w == 0 else down)
            send(c, h, cross[h])
            send(c, h, sibling)

    def cross_step(s):
        for h, way, yy in visits(s):
            c = ctx_of(1 - xl, yy, core)
            arrived(c, h)
            send(c, h, sibling)

    def sibling_wait():
        for xx in (0, 1):
            for yy in range(ny):
                for h in (0, 1):
                    arrived(ctx_of(xx, yy, 1 - core), h)

    def token_signal():
        pl.semaphore_signal(token.at[0], inc=1, device_id=zup, device_id_type=MESH)
        pl.semaphore_signal(token.at[1], inc=1, device_id=zdown, device_id_type=MESH)

    def token_wait():
        pl.semaphore_wait(token.at[0], 1)
        pl.semaphore_wait(token.at[1], 1)

    def exchange(kind, src, dst, k, start):
        i = half_h + (k // 2) * (2 * (k % 2) - 1)
        to = (me_h + i) % nh
        frm = (me_h + nh - i) % nh
        copy = pltpu.make_async_remote_copy(
            src_ref=src(to), dst_ref=dst.at[me_h] if start else dst.at[frm],
            send_sem=xsend.at[kind, to],
            recv_sem=xrecv.at[kind, me_h] if start else xrecv.at[kind, frm],
            device_id=(me_c, to), device_id_type=MESH,
        )
        if start:
            copy.start()
        else:
            copy.wait()
        return 0

    def prepare_small():
        for load in loads[2:6]:
            load.wait()
        gains = jnp.concatenate(
            [gain_in[...].astype(F32), jnp.zeros((128 - iheads, 128), F32)], axis=0
        )
        gains = jnp.transpose(gains).astype(BF16)
        for i in range(8):
            rows = slice(16 * i, 16 * i + 16)
            iq_send[i, :, 0:iheads * 128] = iq_in[rows, :]
            iq_send[i, :, iheads * 128:] = gains[rows, :]
        order = order_in[...]
        blocks = order.shape[1]
        lane = lax.broadcasted_iota(jnp.int32, (1, blocks), 1)
        segs = seg_in[...].astype(F32)
        seg_row = lax.broadcasted_iota(jnp.int32, segs.shape, 0).astype(F32)
        counts = [total_of(jnp.where(segs == float(v), 1.0, 0.0)) for v in range(7)]
        for qb in (0, 1):
            mine_i = jnp.sum(jnp.where(lane == 2 * me_c + qb, order, 0), axis=1, keepdims=True)
            j = lax.broadcasted_iota(jnp.int32, (PAD_J, blocks), 0)
            want = jnp.maximum(mine_i - (reach - 1) + j, 0)
            at = lax.broadcasted_iota(jnp.int32, (PAD_J, blocks), 1)
            slot = jnp.sum(jnp.where(order == want, at, 0), axis=1, keepdims=True)
            slot = jnp.minimum(slot, blocks - 1)
            slot = jnp.broadcast_to(slot, (PAD_J, 128))
            slot_v[0, qb * PAD_J:(qb + 1) * PAD_J, :] = slot
            slot_v[1, qb * PAD_J:(qb + 1) * PAD_J, :] = slot >> 1
            slot_v[2, qb * PAD_J:(qb + 1) * PAD_J, :] = slot & 1
            mine = mine_i.astype(F32)
            first = mine - float(reach - 1)
            pair = jnp.floor(mine * 0.5)
            row = jnp.sum(jnp.where(seg_row == pair, segs, 0.0), axis=0, keepdims=True)
            row = jnp.where(mine - 2.0 * pair > 0.5, pltpu.roll(row, HALF, 1), row)
            sub = lax.broadcasted_iota(jnp.int32, (HALF, 128), 0)
            lan = lax.broadcasted_iota(jnp.int32, (HALF, 128), 1)
            seg_q = jnp.sum(jnp.where(sub == lan, row, 0.0), axis=1, keepdims=True)
            start = jnp.zeros((HALF, 1), F32)
            for v in range(7):
                start = start + jnp.where(seg_q > float(v), counts[v], 0.0)
            pos = mine * float(HALF) + lax.broadcasted_iota(
                jnp.int32, (HALF, 1), 0
            ).astype(F32)
            at = lax.broadcasted_iota(jnp.int32, (HALF, width), 1)
            row_at = lax.broadcasted_iota(jnp.int32, (HALF, width), 0)
            at = at + jnp.where((at < HALF) & (at <= row_at), width, 0)
            kp = first * float(HALF) + at.astype(F32)
            bias[qb] = jnp.where((kp >= start) & (kp <= pos), 0.0, FILL)
        copy = pltpu.make_async_copy(slot_v, slot_s, local.at[7])
        copy.start()
        copy.wait()

    def prepare_queries():
        loads[6].wait()
        for qb in (0, 1):
            for slab in range(4):
                rows = slice(qb * HALF + slab * 16, qb * HALF + slab * 16 + 16)
                for h in range(heads):
                    x = mraw[rows, h * kdim:(h + 1) * kdim]
                    at = slab * 16 * heads + h * 16
                    mq[qb, at:at + 16, 0:LAT] = x[:, 0:LAT]
                    mq[qb, at:at + 16, LAT:] = jnp.concatenate([x[:, LAT:], x[:, LAT:]], axis=1)

    def index_queries():
        def body(i, _):
            exchange(0, lambda to: iq_send.at[to // 2], iq_recv, i, False)
            return 0
        lax.fori_loop(1, nh, body, 0)
        iq_recv[me_h] = iq_send[me_h // 2]
        odd = me_h % 2

        def pick(s, _):
            x = iq_recv[s].astype(F32)
            x = jnp.where(odd == 0, x[0:8], x[8:16])
            at = pl.multiple_of(s * iheads * 8, 16)
            ilhs[pl.ds(at, iheads * 8), :] = jnp.concatenate(
                [x[:, k * 128:(k + 1) * 128] for k in range(iheads)], axis=0
            ).astype(BF16)
            g = x[:, iheads * 128:]
            iwide[pl.ds(at, iheads * 8), :] = jnp.concatenate(
                [jnp.broadcast_to(g[:, k:k + 1], (8, 128)) for k in range(iheads)], axis=0
            )
            return 0

        lax.fori_loop(0, nh, pick, 0)

    mine_qb = me_h // half_h
    mine_row = (me_h % half_h) * 8

    def index_scores():
        rows = ilhs.shape[0]

        def block(j):
            rows = lat[slot_s[1, mine_qb * PAD_J + j, 0]]
            odd = slot_s[2, mine_qb * PAD_J + j, 0]
            lane = lax.broadcasted_iota(jnp.int32, (HALF, 128), 1)
            return jnp.where(
                lane * 0 + odd > 0, rows[:, 2 * kdim + 128:], rows[:, 2 * kdim:2 * kdim + 128]
            )

        def scores(first, count, at):
            ks = [block(first + k) for k in range(count)]
            ks += ks[-1:] * (-count % 2)
            dots = dot_nt(ilhs[...], jnp.concatenate(ks, axis=0))
            for k in range(dots.shape[1] // 128):
                part = jnp.maximum(dots[:, k * 128:(k + 1) * 128], 0.0) * iwide[...]
                part = jnp.sum(part.reshape(rows // 8, 8, 128), axis=0)
                lo = at + k * 128
                if lo < fold:
                    ipack[0:8, lo:lo + 128] = part
                else:
                    ipack[8:16, lo - fold:lo - fold + 128] = part

        for first in range(0, reach - 1, GROUP):
            scores(first, GROUP, first * HALF)
        last = ipack[0:8, 0:128]
        scores(reach - 1, 1, 0)
        lane = lax.broadcasted_iota(jnp.int32, (8, 128), 1)
        row = mine_row + lax.broadcasted_iota(jnp.int32, (8, 128), 0)
        ipack[0:8, 0:128] = jnp.where((lane < HALF) & (lane <= row), ipack[0:8, 0:128], last)

    def packed(x):
        return jnp.concatenate([x[:, 0:fold], x[:, fold:]], axis=0)

    def packed_bias():
        return packed(bias[mine_qb, pl.ds(pl.multiple_of(mine_row, 8), 8), :])

    def both(x, op):
        return op(x[0:8], x[8:16])

    def key_block(qb, j):
        rows = lat[slot_s[1, qb * PAD_J + j, 0]]
        odd = slot_s[2, qb * PAD_J + j, 0]
        lane = lax.broadcasted_iota(jnp.int32, (HALF, 128), 1)
        second = lane * 0 + odd > 0
        second = jnp.concatenate([second] * (LAT // 128), axis=1)
        main = jnp.where(second, rows[:, LAT:2 * LAT], rows[:, 0:LAT])
        tail = rows[:, 2 * LAT:2 * kdim]
        tail = jnp.where(lane // HALF == odd, tail, jnp.zeros_like(tail))
        return jnp.concatenate([main, tail], axis=1)

    def scores_of(qb):
        def body(g, _):
            ks = jnp.concatenate([key_block(qb, g * GROUP + k) for k in range(GROUP)], axis=0)
            at = pl.ds(pl.multiple_of(g * GROUP * HALF, 256), GROUP * HALF)
            score[:, at] = dot_nt(mq[qb], ks)
            return 0

        lax.fori_loop(0, (reach - 1) // GROUP, body, 0, unroll=UNROLL_M)
        last = key_block(qb, reach - 1)
        s = dot_nt(mq[qb], jnp.concatenate([last, last], axis=0))
        at = lax.broadcasted_iota(jnp.int32, s.shape, 0)
        row = at // (16 * heads) * 16 + at % 16
        lane = lax.broadcasted_iota(jnp.int32, s.shape, 1)
        score[:, 0:128] = jnp.where((lane < HALF) & (lane <= row), s, score[:, 0:128])

    def shares_of(qb):
        def slab(i, _):
            b = bias[qb, pl.ds(pl.multiple_of(i * 16, 16), 16), :]
            acc = jnp.zeros((16, width), F32)
            for h in range(heads):
                at = pl.multiple_of(i * (16 * heads) + h * 16, 16)
                s = score[pl.ds(at, 16), :] + b
                top = jnp.max(s, axis=1, keepdims=True)
                p = jnp.exp2((s - top) * EXP_SCALE)
                acc = acc + p * (1.0 / jnp.sum(p, axis=1, keepdims=True))
            for k in (0, 1):
                share = packed(acc[8 * k:8 * k + 8])
                kept[2 * i + k] = share
                tsend[qb * half_h + 2 * i + k] = share.astype(BF16)
            return 0

        lax.fori_loop(0, 4, slab, 0, unroll=4)

        @pl.when(mine_qb == qb)
        def _():
            town[...] = kept[me_h % half_h]

        def share_send(i, _):
            d = qb * half_h + (me_h + i) % half_h

            @pl.when(d != me_h)
            def _():
                pltpu.make_async_remote_copy(
                    src_ref=tsend.at[d], dst_ref=trecv.at[me_h],
                    send_sem=xsend.at[1, d], recv_sem=xrecv.at[1, me_h],
                    device_id=(me_c, d), device_id_type=MESH,
                ).start()

            return 0

        lax.fori_loop(1, half_h + 1, share_send, 0)

    ring_step(0)
    token_signal()
    prepare_small()
    rounds = nz // 2
    token_wait()
    done = 1
    if done < rounds:
        token_signal()
    prepare_queries()
    for s in range(1, far + 1):
        ring_step(s)
        for _ in range(2):
            if done < rounds:
                token_wait()
                done += 1
                if done < rounds:
                    token_signal()
                else:
                    lax.fori_loop(
                        1, nh,
                        lambda i, _: exchange(0, lambda to: iq_send.at[to // 2], iq_recv, i, True),
                        0,
                    )
        cross_step(s - 1)
    cross_step(far)
    sibling_wait()

    for qb in (0, 1):
        scores_of(qb)
        shares_of(qb)

    index_queries()
    index_scores()
    seen_bias = packed_bias()
    index_score = ipack[...]
    masked = index_score + seen_bias
    top = both(jnp.max(masked, axis=1, keepdims=True), jnp.maximum)
    tops = jnp.concatenate([top, top], axis=0)
    exp_sum = both(jnp.sum(jnp.exp(masked - tops), axis=1, keepdims=True), jnp.add)
    lse = top + jnp.log(exp_sum)
    for copy in started:
        copy.wait_send()

    def add_share(i, acc):
        exchange(1, lambda to: tsend.at[to], trecv, i, False)
        return acc + trecv[(me_h + nh - (half_h + (i // 2) * (2 * (i % 2) - 1))) % nh].astype(F32)

    target = lax.fori_loop(1, nh, add_share, town[...]) * (1.0 / HEADS)
    positive = target > 0.0
    logs = jnp.log(jnp.where(positive, target, 1.0))
    gain = both(
        jnp.sum(target * (logs - index_score), axis=1, keepdims=True), jnp.add
    )
    mass = both(jnp.sum(target, axis=1, keepdims=True), jnp.add)
    kl = gain + lse * mass + (1.0 - mass)
    sub = lax.broadcasted_iota(jnp.int32, (8, 128), 0)
    lan = lax.broadcasted_iota(jnp.int32, (8, 128), 1)
    mine = jnp.where(lan == 8 * me_h + sub, kl, 0.0)
    fsend[...] = mine
    lax.fori_loop(1, nh, lambda i, _: exchange(2, lambda to: fsend, frecv, i, True), 0)
    frecv[me_h] = mine
    lax.fori_loop(1, nh, lambda i, _: exchange(2, lambda to: fsend, frecv, i, False), 0)
    out_ref[...] = jnp.sum(jnp.sum(frecv[...], axis=0), axis=0, keepdims=True)


def per_device(
    latent_keys, index_keys, main_query, index_query, index_weight, segment_ids, block_order
):
    rows, kdim = latent_keys.shape
    nc, nh = lax.axis_size("ctx"), lax.axis_size("head")
    ny = nc // 4
    blocks = 2 * nc
    reach = nc // 2 + 1
    heads = main_query.shape[1] // kdim
    iheads = index_weight.shape[1]
    width = (reach - 1) * HALF
    fold = width // 2
    wide = heads * HALF
    half_h = nh // 2
    vmem = pl.BlockSpec(memory_space=pltpu.VMEM)
    hbm = pl.BlockSpec(memory_space=pl.ANY)
    dma = pltpu.SemaphoreType.DMA
    out = pl.pallas_call(
        functools.partial(fused, ny, nh, reach, heads, iheads),
        out_shape=jax.ShapeDtypeStruct((1, rows), F32),
        in_specs=[hbm] * 7,
        out_specs=vmem,
        scratch_shapes=[
            pltpu.VMEM((kdim, rows), BF16),
            pltpu.VMEM((rows, 128), BF16),
            pltpu.VMEM((rows, iheads * 128), BF16),
            pltpu.VMEM((iheads, rows), BF16),
            pltpu.VMEM((blocks * HALF // 128, 128), jnp.int32),
            pltpu.VMEM((1, blocks), jnp.int32),
            pltpu.VMEM((nc, HALF, 2 * kdim + 256), BF16),
            pltpu.VMEM((rows, heads * kdim), BF16),
            pltpu.VMEM((2, wide, LAT + 2 * ROPE), BF16),
            pltpu.VMEM((wide, width), F32),
            pltpu.VMEM((2, HALF, width), F32),
            pltpu.VMEM((8, 16, iheads * 128 + 128), BF16),
            pltpu.VMEM((nh, 16, iheads * 128 + 128), BF16),
            pltpu.VMEM((nh * iheads * 8, 128), BF16),
            pltpu.VMEM((nh * iheads * 8, 128), F32),
            pltpu.VMEM((16, fold), F32),
            pltpu.VMEM((3, 2 * PAD_J, 128), jnp.int32),
            pltpu.SMEM((3, 2 * PAD_J, 128), jnp.int32),
            pltpu.VMEM((nh, 16, fold), BF16),
            pltpu.VMEM((nh, 16, fold), BF16),
            pltpu.VMEM((16, fold), F32),
            pltpu.VMEM((half_h, 16, fold), F32),
            pltpu.VMEM((8, 128), F32),
            pltpu.VMEM((nh, 8, 128), F32),
            dma((2 * (ny - 1) + 6 * ny,)),
            dma((blocks,)),
            dma((3, nh)),
            dma((3, nh)),
            dma((8,)),
            pltpu.SemaphoreType.REGULAR((2,)),
        ],
        compiler_params=pltpu.CompilerParams(
            collective_id=0, has_side_effects=True, vmem_limit_bytes=60 * 2**20
        ),
    )(
        latent_keys.T, index_keys, main_query, index_query, index_weight.T,
        segment_ids.reshape(-1, 128), block_order.reshape(1, blocks),
    )
    return out.reshape(rows)


def solution(mesh):
    in_specs = (
        P("ctx", None),
        P("ctx", None),
        P("ctx", "head"),
        P("ctx", "head"),
        P("ctx", "head"),
        P(),
        P(),
    )
    return jax.shard_map(
        per_device, mesh=mesh, in_specs=in_specs, out_specs=P("ctx"), check_vma=False
    )
```

```python
import functools
import math

import jax
import jax.numpy as jnp
from jax import lax
from jax.experimental import pallas as pl
from jax.experimental.pallas import tpu as pltpu
from jax.sharding import PartitionSpec as P

HEADS = 128
HALF = 64
LAT = 512
ROPE = 64
FILL = -1e30
EXP_SCALE = 192.0 ** (-0.5) * math.log2(math.e)
MESH = pl.DeviceIdType.MESH
NT = (((1,), (1,)), ((), ()))
F32 = jnp.float32
BF16 = jnp.bfloat16
GROUP = 4
UNROLL_M = 4
PAD_J = 24


def dot_nt(a, b):
    return lax.dot_general(a, b, NT, preferred_element_type=F32)


def total_of(x):
    return jnp.sum(jnp.sum(x, axis=1, keepdims=True), axis=0, keepdims=True)


def fused(
    ny, nh, reach, heads, iheads,
    lat_hbm, idx_hbm, mq_hbm, iq_hbm, gain_hbm, seg_hbm, order_hbm,
    out_ref,
    lat_in, idx_in, iq_in, gain_in, seg_in, order_in,
    lat, mraw, mq, score, bias, iq_send, iq_recv, ilhs, iwide, ipack,
    slot_v, slot_s, tsend, trecv, town, kept, fsend, frecv,
    snd, rcv, xsend, xrecv, local, token,
):
    kdim = LAT + ROPE
    me_c, me_h = lax.axis_index("ctx"), lax.axis_index("head")
    core = me_c % 2
    y = (me_c // 2) % ny
    xl = me_c // (2 * ny)
    xh = me_h % 2
    z = me_h // 2
    nz = nh // 2
    far = ny // 2
    half_h = nh // 2
    width = (reach - 1) * HALF
    fold = width // 2

    def ctx_of(xl_, y_, core_):
        return (xl_ * ny + y_) * 2 + core_

    up = (ctx_of(xl, (y + 1) % ny, core), me_h)
    down = (ctx_of(xl, (y + ny - 1) % ny, core), me_h)
    cross = (
        (ctx_of(1 - xl, y, core), me_h),
        (ctx_of(1 - xl, y, core), z * 2 + 1 - xh),
    )
    sibling = (ctx_of(xl, y, 1 - core), me_h)
    zup = (me_c, ((z + 1) % nz) * 2 + xh)
    zdown = (me_c, ((z + nz - 1) % nz) * 2 + xh)
    twin = (me_c, z * 2 + 1 - xh)
    near = (up, down, cross[0], cross[1], sibling, zup, zdown, twin)

    loads = [
        pltpu.make_async_copy(src, dst, local.at[i])
        for i, (src, dst) in enumerate(
            [
                (lat_hbm, lat_in), (idx_hbm, idx_in), (iq_hbm, iq_in), (gain_hbm, gain_in),
                (seg_hbm, seg_in), (order_hbm, order_in), (mq_hbm, mraw),
            ]
        )
    ]
    for load in loads:
        load.start()
    barrier = pltpu.get_barrier_semaphore()
    for dev in near:
        pl.semaphore_signal(barrier, inc=1, device_id=dev, device_id_type=MESH)

    own = ctx_of(xl, y, core)
    loads[0].wait()
    loads[1].wait()
    keys = jnp.transpose(lat_in[...])
    lat[own, :, 0:LAT] = keys[0:HALF, 0:LAT]
    lat[own, :, LAT:2 * LAT] = keys[HALF:, 0:LAT]
    lat[own, :, 2 * LAT:2 * kdim] = jnp.concatenate([keys[0:HALF, LAT:], keys[HALF:, LAT:]], axis=1)
    for h in (0, 1):
        at = 2 * kdim + h * 128
        lat[own, :, at:at + 128] = idx_in[h * HALF:(h + 1) * HALF, :]

    pl.semaphore_wait(barrier, len(near))

    started = []

    def piece(c, h):
        return lat.at[c, pl.ds(h * (HALF // 2), HALF // 2)], rcv.at[c * 2 + h]

    def send(c, h, dev):
        ref, sem = piece(c, h)
        copy = pltpu.make_async_remote_copy(
            src_ref=ref, dst_ref=ref, send_sem=snd.at[len(started)], recv_sem=sem,
            device_id=dev, device_id_type=MESH,
        )
        copy.start()
        started.append(copy)

    def arrived(c, h):
        ref, sem = piece(c, h)
        pltpu.make_async_remote_copy(
            src_ref=ref, dst_ref=ref, send_sem=snd.at[0], recv_sem=sem,
            device_id=sibling, device_id_type=MESH,
        ).wait_recv()

    def goes(dist, h, way):
        return dist < far or (dist == far and h == way)

    def visits(s):
        for h in (0, 1):
            for way in (0, 1):
                if s == 0 and way == 1:
                    continue
                if s > 0 and not goes(s, h, way):
                    continue
                yield h, way, (y + ny - s) % ny if way == 0 else (y + s) % ny

    def ring_step(s):
        for h, way, yy in visits(s):
            c = ctx_of(xl, yy, core)
            if s > 0:
                arrived(c, h)
            for w in ((0, 1) if s == 0 else (way,)):
                if goes(s + 1, h, w):
                    send(c, h, up if w == 0 else down)
            send(c, h, cross[h])
            send(c, h, sibling)

    def cross_step(s):
        for h, way, yy in visits(s):
            c = ctx_of(1 - xl, yy, core)
            arrived(c, h)
            send(c, h, sibling)

    def sibling_wait():
        for xx in (0, 1):
            for yy in range(ny):
                for h in (0, 1):
                    arrived(ctx_of(xx, yy, 1 - core), h)

    def token_signal():
        pl.semaphore_signal(token.at[0], inc=1, device_id=zup, device_id_type=MESH)
        pl.semaphore_signal(token.at[1], inc=1, device_id=zdown, device_id_type=MESH)

    def token_wait():
        pl.semaphore_wait(token.at[0], 1)
        pl.semaphore_wait(token.at[1], 1)

    def spread(k):
        return half_h + lax.div(k, 2) * (2 * lax.rem(k, 2) - 1)

    def exchange(kind, src, dst, k, start):
        i = spread(k)
        to = lax.rem(me_h + i, nh)
        frm = lax.rem(me_h + nh - i, nh)
        copy = pltpu.make_async_remote_copy(
            src_ref=src(to), dst_ref=dst.at[me_h] if start else dst.at[frm],
            send_sem=xsend.at[kind, to],
            recv_sem=xrecv.at[kind, me_h] if start else xrecv.at[kind, frm],
            device_id=(me_c, to), device_id_type=MESH,
        )
        if start:
            copy.start()
        else:
            copy.wait()
        return 0

    def prepare_small():
        for load in loads[2:6]:
            load.wait()
        gains = jnp.concatenate(
            [gain_in[...].astype(F32), jnp.zeros((128 - iheads, 128), F32)], axis=0
        )
        gains = jnp.transpose(gains).astype(BF16)
        for i in range(8):
            rows = slice(16 * i, 16 * i + 16)
            iq_send[i, :, 0:iheads * 128] = iq_in[rows, :]
            iq_send[i, :, iheads * 128:] = gains[rows, :]
        order = order_in[...]
        blocks = order.shape[1]
        lane = lax.broadcasted_iota(jnp.int32, (1, blocks), 1)
        segs = seg_in[...].astype(F32)
        seg_row = lax.broadcasted_iota(jnp.int32, segs.shape, 0).astype(F32)
        counts = [total_of(jnp.where(segs == float(v), 1.0, 0.0)) for v in range(7)]
        for qb in (0, 1):
            mine_i = jnp.sum(jnp.where(lane == 2 * me_c + qb, order, 0), axis=1, keepdims=True)
            j = lax.broadcasted_iota(jnp.int32, (PAD_J, blocks), 0)
            want = jnp.maximum(mine_i - (reach - 1) + j, 0)
            at = lax.broadcasted_iota(jnp.int32, (PAD_J, blocks), 1)
            slot = jnp.sum(jnp.where(order == want, at, 0), axis=1, keepdims=True)
            slot = jnp.minimum(slot, blocks - 1)
            slot = jnp.broadcast_to(slot, (PAD_J, 128))
            slot_v[0, qb * PAD_J:(qb + 1) * PAD_J, :] = slot
            slot_v[1, qb * PAD_J:(qb + 1) * PAD_J, :] = slot >> 1
            slot_v[2, qb * PAD_J:(qb + 1) * PAD_J, :] = slot & 1
            mine = mine_i.astype(F32)
            first = mine - float(reach - 1)
            pair = jnp.floor(mine * 0.5)
            row = jnp.sum(jnp.where(seg_row == pair, segs, 0.0), axis=0, keepdims=True)
            row = jnp.where(mine - 2.0 * pair > 0.5, pltpu.roll(row, HALF, 1), row)
            sub = lax.broadcasted_iota(jnp.int32, (HALF, 128), 0)
            lan = lax.broadcasted_iota(jnp.int32, (HALF, 128), 1)
            seg_q = jnp.sum(jnp.where(sub == lan, row, 0.0), axis=1, keepdims=True)
            start = jnp.zeros((HALF, 1), F32)
            for v in range(7):
                start = start + jnp.where(seg_q > float(v), counts[v], 0.0)
            pos = mine * float(HALF) + lax.broadcasted_iota(
                jnp.int32, (HALF, 1), 0
            ).astype(F32)
            at = lax.broadcasted_iota(jnp.int32, (HALF, width), 1)
            row_at = lax.broadcasted_iota(jnp.int32, (HALF, width), 0)
            at = at + jnp.where((at < HALF) & (at <= row_at), width, 0)
            kp = first * float(HALF) + at.astype(F32)
            bias[qb] = jnp.where((kp >= start) & (kp <= pos), 0.0, FILL)
        copy = pltpu.make_async_copy(slot_v, slot_s, local.at[7])
        copy.start()
        copy.wait()

    def prepare_queries():
        loads[6].wait()
        for qb in (0, 1):
            for slab in range(4):
                rows = slice(qb * HALF + slab * 16, qb * HALF + slab * 16 + 16)
                for h in range(heads):
                    x = mraw[rows, h * kdim:(h + 1) * kdim]
                    at = slab * 16 * heads + h * 16
                    mq[qb, at:at + 16, 0:LAT] = x[:, 0:LAT]
                    mq[qb, at:at + 16, LAT:] = jnp.concatenate([x[:, LAT:], x[:, LAT:]], axis=1)

    def index_queries():
        def body(i, _):
            exchange(0, lambda to: iq_send.at[to // 2], iq_recv, i, False)
            return 0
        lax.fori_loop(1, nh, body, 0)
        iq_recv[me_h] = iq_send[me_h // 2]
        odd = me_h % 2

        def pick(s, _):
            x = iq_recv[s].astype(F32)
            x = jnp.where(odd == 0, x[0:8], x[8:16])
            at = pl.multiple_of(s * iheads * 8, 16)
            ilhs[pl.ds(at, iheads * 8), :] = jnp.concatenate(
                [x[:, k * 128:(k + 1) * 128] for k in range(iheads)], axis=0
            ).astype(BF16)
            g = x[:, iheads * 128:]
            iwide[pl.ds(at, iheads * 8), :] = jnp.concatenate(
                [jnp.broadcast_to(g[:, k:k + 1], (8, 128)) for k in range(iheads)], axis=0
            )
            return 0

        lax.fori_loop(0, nh, pick, 0)

    mine_qb = me_h // half_h
    mine_row = (me_h % half_h) * 8

    def index_scores():
        rows = ilhs.shape[0]

        def block(j):
            rows = lat[slot_s[1, mine_qb * PAD_J + j, 0]]
            odd = slot_s[2, mine_qb * PAD_J + j, 0]
            lane = lax.broadcasted_iota(jnp.int32, (HALF, 128), 1)
            return jnp.where(
                lane * 0 + odd > 0, rows[:, 2 * kdim + 128:], rows[:, 2 * kdim:2 * kdim + 128]
            )

        def scores(first, count, at):
            ks = [block(first + k) for k in range(count)]
            ks += ks[-1:] * (-count % 2)
            dots = dot_nt(ilhs[...], jnp.concatenate(ks, axis=0))
            for k in range(dots.shape[1] // 128):
                part = jnp.maximum(dots[:, k * 128:(k + 1) * 128], 0.0) * iwide[...]
                part = jnp.sum(part.reshape(rows // 8, 8, 128), axis=0)
                lo = at + k * 128
                if lo < fold:
                    ipack[0:8, lo:lo + 128] = part
                else:
                    ipack[8:16, lo - fold:lo - fold + 128] = part

        for first in range(0, reach - 1, GROUP):
            scores(first, GROUP, first * HALF)
        last = ipack[0:8, 0:128]
        scores(reach - 1, 1, 0)
        lane = lax.broadcasted_iota(jnp.int32, (8, 128), 1)
        row = mine_row + lax.broadcasted_iota(jnp.int32, (8, 128), 0)
        ipack[0:8, 0:128] = jnp.where((lane < HALF) & (lane <= row), ipack[0:8, 0:128], last)

    def packed(x):
        return jnp.concatenate([x[:, 0:fold], x[:, fold:]], axis=0)

    def packed_bias():
        return packed(bias[mine_qb, pl.ds(pl.multiple_of(mine_row, 8), 8), :])

    def both(x, op):
        return op(x[0:8], x[8:16])

    def key_block(qb, j):
        rows = lat[slot_s[1, qb * PAD_J + j, 0]]
        odd = slot_s[2, qb * PAD_J + j, 0]
        lane = lax.broadcasted_iota(jnp.int32, (HALF, 128), 1)
        second = lane * 0 + odd > 0
        second = jnp.concatenate([second] * (LAT // 128), axis=1)
        main = jnp.where(second, rows[:, LAT:2 * LAT], rows[:, 0:LAT])
        tail = rows[:, 2 * LAT:2 * kdim]
        tail = jnp.where(lane // HALF == odd, tail, jnp.zeros_like(tail))
        return jnp.concatenate([main, tail], axis=1)

    def scores_of(qb):
        def body(g, _):
            ks = jnp.concatenate([key_block(qb, g * GROUP + k) for k in range(GROUP)], axis=0)
            at = pl.ds(pl.multiple_of(g * GROUP * HALF, 256), GROUP * HALF)
            score[:, at] = dot_nt(mq[qb], ks)
            return 0

        lax.fori_loop(0, (reach - 1) // GROUP, body, 0, unroll=UNROLL_M)
        last = key_block(qb, reach - 1)
        s = dot_nt(mq[qb], jnp.concatenate([last, last], axis=0))
        at = lax.broadcasted_iota(jnp.int32, s.shape, 0)
        row = at // (16 * heads) * 16 + at % 16
        lane = lax.broadcasted_iota(jnp.int32, s.shape, 1)
        score[:, 0:128] = jnp.where((lane < HALF) & (lane <= row), s, score[:, 0:128])

    def shares_of(qb):
        def slab(i, _):
            b = bias[qb, pl.ds(pl.multiple_of(i * 16, 16), 16), :]
            acc = jnp.zeros((16, width), F32)
            for h in range(heads):
                at = pl.multiple_of(i * (16 * heads) + h * 16, 16)
                s = score[pl.ds(at, 16), :] + b
                top = jnp.max(s, axis=1, keepdims=True)
                p = jnp.exp2((s - top) * EXP_SCALE)
                acc = acc + p * (1.0 / jnp.sum(p, axis=1, keepdims=True))
            for k in (0, 1):
                share = packed(acc[8 * k:8 * k + 8])
                kept[2 * i + k] = share
                tsend[qb * half_h + 2 * i + k] = share.astype(BF16)
            return 0

        lax.fori_loop(0, 4, slab, 0, unroll=4)

        @pl.when(mine_qb == qb)
        def _():
            town[...] = kept[me_h % half_h]

        def share_send(i, _):
            d = qb * half_h + (me_h + i) % half_h

            @pl.when(d != me_h)
            def _():
                pltpu.make_async_remote_copy(
                    src_ref=tsend.at[d], dst_ref=trecv.at[me_h],
                    send_sem=xsend.at[1, d], recv_sem=xrecv.at[1, me_h],
                    device_id=(me_c, d), device_id_type=MESH,
                ).start()

            return 0

        lax.fori_loop(1, half_h + 1, share_send, 0)

    ring_step(0)
    token_signal()
    prepare_small()
    rounds = nz // 2
    token_wait()
    done = 1
    if done < rounds:
        token_signal()
    prepare_queries()
    for s in range(1, far + 1):
        ring_step(s)
        for _ in range(2):
            if done < rounds:
                token_wait()
                done += 1
                if done < rounds:
                    token_signal()
                else:
                    lax.fori_loop(
                        1, nh,
                        lambda i, _: exchange(0, lambda to: iq_send.at[to // 2], iq_recv, i, True),
                        0,
                    )
        cross_step(s - 1)
    index_queries()
    cross_step(far)
    sibling_wait()

    for qb in (0, 1):
        scores_of(qb)
        shares_of(qb)

    index_scores()
    seen_bias = packed_bias()
    index_score = ipack[...]
    masked = index_score + seen_bias
    top = both(jnp.max(masked, axis=1, keepdims=True), jnp.maximum)
    tops = jnp.concatenate([top, top], axis=0)
    exp_sum = both(jnp.sum(jnp.exp(masked - tops), axis=1, keepdims=True), jnp.add)
    lse = top + jnp.log(exp_sum)
    for copy in started:
        copy.wait_send()

    def add_share(i, acc):
        exchange(1, lambda to: tsend.at[to], trecv, nh - i, False)
        return acc + trecv[lax.rem(me_h + nh - spread(nh - i), nh)].astype(F32)

    target = lax.fori_loop(1, nh, add_share, town[...]) * (1.0 / HEADS)
    positive = target > 0.0
    logs = jnp.log(jnp.where(positive, target, 1.0))
    gain = both(
        jnp.sum(target * (logs - index_score), axis=1, keepdims=True), jnp.add
    )
    mass = both(jnp.sum(target, axis=1, keepdims=True), jnp.add)
    kl = gain + lse * mass + (1.0 - mass)
    sub = lax.broadcasted_iota(jnp.int32, (8, 128), 0)
    lan = lax.broadcasted_iota(jnp.int32, (8, 128), 1)
    mine = jnp.where(lan == 8 * me_h + sub, kl, 0.0)
    fsend[...] = mine
    lax.fori_loop(1, nh, lambda i, _: exchange(2, lambda to: fsend, frecv, i, True), 0)
    frecv[me_h] = mine
    lax.fori_loop(1, nh, lambda i, _: exchange(2, lambda to: fsend, frecv, i, False), 0)
    out_ref[...] = jnp.sum(jnp.sum(frecv[...], axis=0), axis=0, keepdims=True)


def per_device(
    latent_keys, index_keys, main_query, index_query, index_weight, segment_ids, block_order
):
    rows, kdim = latent_keys.shape
    nc, nh = lax.axis_size("ctx"), lax.axis_size("head")
    ny = nc // 4
    blocks = 2 * nc
    reach = nc // 2 + 1
    heads = main_query.shape[1] // kdim
    iheads = index_weight.shape[1]
    width = (reach - 1) * HALF
    fold = width // 2
    wide = heads * HALF
    half_h = nh // 2
    vmem = pl.BlockSpec(memory_space=pltpu.VMEM)
    hbm = pl.BlockSpec(memory_space=pl.ANY)
    dma = pltpu.SemaphoreType.DMA
    out = pl.pallas_call(
        functools.partial(fused, ny, nh, reach, heads, iheads),
        out_shape=jax.ShapeDtypeStruct((1, rows), F32),
        in_specs=[hbm] * 7,
        out_specs=vmem,
        scratch_shapes=[
            pltpu.VMEM((kdim, rows), BF16),
            pltpu.VMEM((rows, 128), BF16),
            pltpu.VMEM((rows, iheads * 128), BF16),
            pltpu.VMEM((iheads, rows), BF16),
            pltpu.VMEM((blocks * HALF // 128, 128), jnp.int32),
            pltpu.VMEM((1, blocks), jnp.int32),
            pltpu.VMEM((nc, HALF, 2 * kdim + 256), BF16),
            pltpu.VMEM((rows, heads * kdim), BF16),
            pltpu.VMEM((2, wide, LAT + 2 * ROPE), BF16),
            pltpu.VMEM((wide, width), F32),
            pltpu.VMEM((2, HALF, width), F32),
            pltpu.VMEM((8, 16, iheads * 128 + 128), BF16),
            pltpu.VMEM((nh, 16, iheads * 128 + 128), BF16),
            pltpu.VMEM((nh * iheads * 8, 128), BF16),
            pltpu.VMEM((nh * iheads * 8, 128), F32),
            pltpu.VMEM((16, fold), F32),
            pltpu.VMEM((3, 2 * PAD_J, 128), jnp.int32),
            pltpu.SMEM((3, 2 * PAD_J, 128), jnp.int32),
            pltpu.VMEM((nh, 16, fold), BF16),
            pltpu.VMEM((nh, 16, fold), BF16),
            pltpu.VMEM((16, fold), F32),
            pltpu.VMEM((half_h, 16, fold), F32),
            pltpu.VMEM((8, 128), F32),
            pltpu.VMEM((nh, 8, 128), F32),
            dma((2 * (ny - 1) + 6 * ny,)),
            dma((blocks,)),
            dma((3, nh)),
            dma((3, nh)),
            dma((8,)),
            pltpu.SemaphoreType.REGULAR((2,)),
        ],
        compiler_params=pltpu.CompilerParams(
            collective_id=0, has_side_effects=True, vmem_limit_bytes=60 * 2**20
        ),
    )(
        latent_keys.T, index_keys, main_query, index_query, index_weight.T,
        segment_ids.reshape(-1, 128), block_order.reshape(1, blocks),
    )
    return out.reshape(rows)


def solution(mesh):
    in_specs = (
        P("ctx", None),
        P("ctx", None),
        P("ctx", "head"),
        P("ctx", "head"),
        P("ctx", "head"),
        P(),
        P(),
    )
    return jax.shard_map(
        per_device, mesh=mesh, in_specs=in_specs, out_specs=P("ctx"), check_vma=False
    )
```

```python
import functools
import math

import jax
import jax.numpy as jnp
from jax import lax
from jax.experimental import pallas as pl
from jax.experimental.pallas import tpu as pltpu
from jax.sharding import PartitionSpec as P

HEADS = 128
HALF = 64
LAT = 512
ROPE = 64
FILL = -1e30
EXP_SCALE = 192.0 ** (-0.5) * math.log2(math.e)
MESH = pl.DeviceIdType.MESH
NT = (((1,), (1,)), ((), ()))
F32 = jnp.float32
BF16 = jnp.bfloat16
GROUP = 4
UNROLL_M = 4
PAD_J = 24


def dot_nt(a, b):
    return lax.dot_general(a, b, NT, preferred_element_type=F32)


def total_of(x):
    return jnp.sum(jnp.sum(x, axis=1, keepdims=True), axis=0, keepdims=True)


def fused(
    ny, nh, reach, heads, iheads,
    lat_hbm, idx_hbm, mq_hbm, iq_hbm, gain_hbm, seg_hbm, order_hbm,
    out_ref,
    lat_in, idx_in, iq_in, gain_in, seg_in, order_in,
    lat, mraw, mq, score, bias, iq_send, iq_recv, ilhs, iwide, ipack,
    slot_v, slot_s, tsend, trecv, town, kept, fsend, frecv,
    snd, rcv, xsend, xrecv, local, token,
):
    kdim = LAT + ROPE
    me_c, me_h = lax.axis_index("ctx"), lax.axis_index("head")
    core = me_c % 2
    y = (me_c // 2) % ny
    xl = me_c // (2 * ny)
    xh = me_h % 2
    z = me_h // 2
    nz = nh // 2
    far = ny // 2
    half_h = nh // 2
    width = (reach - 1) * HALF
    fold = width // 2

    def ctx_of(xl_, y_, core_):
        return (xl_ * ny + y_) * 2 + core_

    up = (ctx_of(xl, (y + 1) % ny, core), me_h)
    down = (ctx_of(xl, (y + ny - 1) % ny, core), me_h)
    cross = (
        (ctx_of(1 - xl, y, core), me_h),
        (ctx_of(1 - xl, y, core), z * 2 + 1 - xh),
    )
    sibling = (ctx_of(xl, y, 1 - core), me_h)
    zup = (me_c, ((z + 1) % nz) * 2 + xh)
    zdown = (me_c, ((z + nz - 1) % nz) * 2 + xh)
    twin = (me_c, z * 2 + 1 - xh)
    near = (up, down, cross[0], cross[1], sibling, zup, zdown, twin)

    loads = [
        pltpu.make_async_copy(src, dst, local.at[i])
        for i, (src, dst) in enumerate(
            [
                (lat_hbm, lat_in), (idx_hbm, idx_in), (iq_hbm, iq_in), (gain_hbm, gain_in),
                (seg_hbm, seg_in), (order_hbm, order_in), (mq_hbm, mraw),
            ]
        )
    ]
    for load in loads:
        load.start()
    barrier = pltpu.get_barrier_semaphore()
    for dev in near:
        pl.semaphore_signal(barrier, inc=1, device_id=dev, device_id_type=MESH)

    own = ctx_of(xl, y, core)
    loads[0].wait()
    loads[1].wait()
    keys = jnp.transpose(lat_in[...])
    lat[own, :, 0:LAT] = keys[0:HALF, 0:LAT]
    lat[own, :, LAT:2 * LAT] = keys[HALF:, 0:LAT]
    lat[own, :, 2 * LAT:2 * kdim] = jnp.concatenate([keys[0:HALF, LAT:], keys[HALF:, LAT:]], axis=1)
    for h in (0, 1):
        at = 2 * kdim + h * 128
        lat[own, :, at:at + 128] = idx_in[h * HALF:(h + 1) * HALF, :]

    pl.semaphore_wait(barrier, len(near))

    started = []

    def piece(c, h):
        return lat.at[c, pl.ds(h * (HALF // 2), HALF // 2)], rcv.at[c * 2 + h]

    def send(c, h, dev):
        ref, sem = piece(c, h)
        copy = pltpu.make_async_remote_copy(
            src_ref=ref, dst_ref=ref, send_sem=snd.at[len(started)], recv_sem=sem,
            device_id=dev, device_id_type=MESH,
        )
        copy.start()
        started.append(copy)

    def arrived(c, h):
        ref, sem = piece(c, h)
        pltpu.make_async_remote_copy(
            src_ref=ref, dst_ref=ref, send_sem=snd.at[0], recv_sem=sem,
            device_id=sibling, device_id_type=MESH,
        ).wait_recv()

    def goes(dist, h, way):
        return dist < far or (dist == far and h == way)

    def visits(s):
        for h in (0, 1):
            for way in (0, 1):
                if s == 0 and way == 1:
                    continue
                if s > 0 and not goes(s, h, way):
                    continue
                yield h, way, (y + ny - s) % ny if way == 0 else (y + s) % ny

    def ring_step(s):
        for h, way, yy in visits(s):
            c = ctx_of(xl, yy, core)
            if s > 0:
                arrived(c, h)
            for w in ((0, 1) if s == 0 else (way,)):
                if goes(s + 1, h, w):
                    send(c, h, up if w == 0 else down)
            send(c, h, cross[h])
            send(c, h, sibling)

    def cross_step(s):
        for h, way, yy in visits(s):
            c = ctx_of(1 - xl, yy, core)
            arrived(c, h)
            send(c, h, sibling)

    def sibling_wait():
        for xx in (0, 1):
            for yy in range(ny):
                for h in (0, 1):
                    arrived(ctx_of(xx, yy, 1 - core), h)

    def token_signal():
        pl.semaphore_signal(token.at[0], inc=1, device_id=zup, device_id_type=MESH)
        pl.semaphore_signal(token.at[1], inc=1, device_id=zdown, device_id_type=MESH)

    def token_wait():
        pl.semaphore_wait(token.at[0], 1)
        pl.semaphore_wait(token.at[1], 1)

    def spread(k):
        return half_h + lax.div(k, 2) * (2 * lax.rem(k, 2) - 1)

    def exchange(kind, src, dst, k, start):
        i = spread(k)
        to = lax.rem(me_h + i, nh)
        frm = lax.rem(me_h + nh - i, nh)
        copy = pltpu.make_async_remote_copy(
            src_ref=src(to), dst_ref=dst.at[me_h] if start else dst.at[frm],
            send_sem=xsend.at[kind, to],
            recv_sem=xrecv.at[kind, me_h] if start else xrecv.at[kind, frm],
            device_id=(me_c, to), device_id_type=MESH,
        )
        if start:
            copy.start()
        else:
            copy.wait()
        return 0

    def prepare_small():
        for load in loads[2:6]:
            load.wait()
        gains = jnp.concatenate(
            [gain_in[...].astype(F32), jnp.zeros((128 - iheads, 128), F32)], axis=0
        )
        gains = jnp.transpose(gains).astype(BF16)
        for i in range(8):
            rows = slice(16 * i, 16 * i + 16)
            iq_send[i, :, 0:iheads * 128] = iq_in[rows, :]
            iq_send[i, :, iheads * 128:] = gains[rows, :]
        order = order_in[...]
        blocks = order.shape[1]
        lane = lax.broadcasted_iota(jnp.int32, (1, blocks), 1)
        segs = seg_in[...].astype(F32)
        seg_row = lax.broadcasted_iota(jnp.int32, segs.shape, 0).astype(F32)
        counts = [total_of(jnp.where(segs == float(v), 1.0, 0.0)) for v in range(7)]
        for qb in (0, 1):
            mine_i = jnp.sum(jnp.where(lane == 2 * me_c + qb, order, 0), axis=1, keepdims=True)
            j = lax.broadcasted_iota(jnp.int32, (PAD_J, blocks), 0)
            want = jnp.maximum(mine_i - (reach - 1) + j, 0)
            at = lax.broadcasted_iota(jnp.int32, (PAD_J, blocks), 1)
            slot = jnp.sum(jnp.where(order == want, at, 0), axis=1, keepdims=True)
            slot = jnp.minimum(slot, blocks - 1)
            slot = jnp.broadcast_to(slot, (PAD_J, 128))
            slot_v[0, qb * PAD_J:(qb + 1) * PAD_J, :] = slot
            slot_v[1, qb * PAD_J:(qb + 1) * PAD_J, :] = slot >> 1
            slot_v[2, qb * PAD_J:(qb + 1) * PAD_J, :] = slot & 1
            mine = mine_i.astype(F32)
            first = mine - float(reach - 1)
            pair = jnp.floor(mine * 0.5)
            row = jnp.sum(jnp.where(seg_row == pair, segs, 0.0), axis=0, keepdims=True)
            row = jnp.where(mine - 2.0 * pair > 0.5, pltpu.roll(row, HALF, 1), row)
            sub = lax.broadcasted_iota(jnp.int32, (HALF, 128), 0)
            lan = lax.broadcasted_iota(jnp.int32, (HALF, 128), 1)
            seg_q = jnp.sum(jnp.where(sub == lan, row, 0.0), axis=1, keepdims=True)
            start = jnp.zeros((HALF, 1), F32)
            for v in range(7):
                start = start + jnp.where(seg_q > float(v), counts[v], 0.0)
            pos = mine * float(HALF) + lax.broadcasted_iota(
                jnp.int32, (HALF, 1), 0
            ).astype(F32)
            at = lax.broadcasted_iota(jnp.int32, (HALF, width), 1)
            row_at = lax.broadcasted_iota(jnp.int32, (HALF, width), 0)
            at = at + jnp.where((at < HALF) & (at <= row_at), width, 0)
            kp = first * float(HALF) + at.astype(F32)
            bias[qb] = jnp.where((kp >= start) & (kp <= pos), 0.0, FILL)
        copy = pltpu.make_async_copy(slot_v, slot_s, local.at[7])
        copy.start()
        copy.wait()

    def prepare_queries():
        loads[6].wait()
        for qb in (0, 1):
            for slab in range(4):
                rows = slice(qb * HALF + slab * 16, qb * HALF + slab * 16 + 16)
                for h in range(heads):
                    x = mraw[rows, h * kdim:(h + 1) * kdim]
                    at = slab * 16 * heads + h * 16
                    mq[qb, at:at + 16, 0:LAT] = x[:, 0:LAT]
                    mq[qb, at:at + 16, LAT:] = jnp.concatenate([x[:, LAT:], x[:, LAT:]], axis=1)

    def index_queries():
        def body(i, _):
            exchange(0, lambda to: iq_send.at[to // 2], iq_recv, i, False)
            return 0
        lax.fori_loop(1, nh, body, 0)
        iq_recv[me_h] = iq_send[me_h // 2]
        odd = me_h % 2

        def pick(s, _):
            x = iq_recv[s].astype(F32)
            x = jnp.where(odd == 0, x[0:8], x[8:16])
            at = pl.multiple_of(s * iheads * 8, 16)
            ilhs[pl.ds(at, iheads * 8), :] = jnp.concatenate(
                [x[:, k * 128:(k + 1) * 128] for k in range(iheads)], axis=0
            ).astype(BF16)
            g = x[:, iheads * 128:]
            iwide[pl.ds(at, iheads * 8), :] = jnp.concatenate(
                [jnp.broadcast_to(g[:, k:k + 1], (8, 128)) for k in range(iheads)], axis=0
            )
            return 0

        lax.fori_loop(0, nh, pick, 0)

    mine_qb = me_h // half_h
    mine_row = (me_h % half_h) * 8

    def index_scores():
        rows = ilhs.shape[0]

        def block(j):
            rows = lat[slot_s[1, mine_qb * PAD_J + j, 0]]
            odd = slot_s[2, mine_qb * PAD_J + j, 0]
            lane = lax.broadcasted_iota(jnp.int32, (HALF, 128), 1)
            return jnp.where(
                lane * 0 + odd > 0, rows[:, 2 * kdim + 128:], rows[:, 2 * kdim:2 * kdim + 128]
            )

        def scores(first, count, at):
            ks = [block(first + k) for k in range(count)]
            ks += ks[-1:] * (-count % 2)
            dots = dot_nt(ilhs[...], jnp.concatenate(ks, axis=0))
            for k in range(dots.shape[1] // 128):
                part = jnp.maximum(dots[:, k * 128:(k + 1) * 128], 0.0) * iwide[...]
                part = jnp.sum(part.reshape(rows // 8, 8, 128), axis=0)
                lo = at + k * 128
                if lo < fold:
                    ipack[0:8, lo:lo + 128] = part
                else:
                    ipack[8:16, lo - fold:lo - fold + 128] = part

        for first in range(0, reach - 1, GROUP):
            scores(first, GROUP, first * HALF)
        last = ipack[0:8, 0:128]
        scores(reach - 1, 1, 0)
        lane = lax.broadcasted_iota(jnp.int32, (8, 128), 1)
        row = mine_row + lax.broadcasted_iota(jnp.int32, (8, 128), 0)
        ipack[0:8, 0:128] = jnp.where((lane < HALF) & (lane <= row), ipack[0:8, 0:128], last)

    def packed(x):
        return jnp.concatenate([x[:, 0:fold], x[:, fold:]], axis=0)

    def packed_bias():
        return packed(bias[mine_qb, pl.ds(pl.multiple_of(mine_row, 8), 8), :])

    def both(x, op):
        return op(x[0:8], x[8:16])

    def key_block(qb, j):
        rows = lat[slot_s[1, qb * PAD_J + j, 0]]
        odd = slot_s[2, qb * PAD_J + j, 0]
        lane = lax.broadcasted_iota(jnp.int32, (HALF, 128), 1)
        second = lane * 0 + odd > 0
        second = jnp.concatenate([second] * (LAT // 128), axis=1)
        main = jnp.where(second, rows[:, LAT:2 * LAT], rows[:, 0:LAT])
        tail = rows[:, 2 * LAT:2 * kdim]
        tail = jnp.where(lane // HALF == odd, tail, jnp.zeros_like(tail))
        return jnp.concatenate([main, tail], axis=1)

    def scores_of(qb):
        def body(g, _):
            ks = jnp.concatenate([key_block(qb, g * GROUP + k) for k in range(GROUP)], axis=0)
            at = pl.ds(pl.multiple_of(g * GROUP * HALF, 256), GROUP * HALF)
            score[:, at] = dot_nt(mq[qb], ks)
            return 0

        lax.fori_loop(0, (reach - 1) // GROUP, body, 0, unroll=UNROLL_M)
        last = key_block(qb, reach - 1)
        s = dot_nt(mq[qb], jnp.concatenate([last, last], axis=0))
        at = lax.broadcasted_iota(jnp.int32, s.shape, 0)
        row = at // (16 * heads) * 16 + at % 16
        lane = lax.broadcasted_iota(jnp.int32, s.shape, 1)
        score[:, 0:128] = jnp.where((lane < HALF) & (lane <= row), s, score[:, 0:128])

    def shares_of(qb, mine):
        def slab(i, _):
            b = bias[qb, pl.ds(pl.multiple_of(i * 16, 16), 16), :]
            acc = jnp.zeros((16, width), F32)
            for h in range(heads):
                at = pl.multiple_of(i * (16 * heads) + h * 16, 16)
                s = score[pl.ds(at, 16), :] + b
                top = jnp.max(s, axis=1, keepdims=True)
                p = jnp.exp2((s - top) * EXP_SCALE)
                acc = acc + p * (1.0 / jnp.sum(p, axis=1, keepdims=True))
            for k in (0, 1):
                share = packed(acc[8 * k:8 * k + 8])
                kept[2 * i + k] = share
                tsend[qb * half_h + 2 * i + k] = share.astype(BF16)
            return 0

        lax.fori_loop(0, 4, slab, 0, unroll=4)

        here = lax.rem(me_h, half_h)
        if mine:
            town[...] = kept[here]

        def share_send(k, _):
            if mine:
                off = half_h // 2 + lax.div(k, 2) * (2 * lax.rem(k, 2) - 1)
            else:
                off = lax.div(k + 1, 2) * (1 - 2 * lax.rem(k, 2))
            d = qb * half_h + lax.rem(here + half_h + off, half_h)
            pltpu.make_async_remote_copy(
                src_ref=tsend.at[d], dst_ref=trecv.at[me_h],
                send_sem=xsend.at[1, d], recv_sem=xrecv.at[1, me_h],
                device_id=(me_c, d), device_id_type=MESH,
            ).start()
            return 0

        lax.fori_loop(1 if mine else 0, half_h, share_send, 0)

    ring_step(0)
    token_signal()
    prepare_small()
    rounds = nz // 2
    token_wait()
    done = 1
    if done < rounds:
        token_signal()
    prepare_queries()
    for s in range(1, far + 1):
        ring_step(s)
        for _ in range(2):
            if done < rounds:
                token_wait()
                done += 1
                if done < rounds:
                    token_signal()
                else:
                    lax.fori_loop(
                        1, nh,
                        lambda i, _: exchange(0, lambda to: iq_send.at[to // 2], iq_recv, i, True),
                        0,
                    )
        cross_step(s - 1)
    index_queries()
    cross_step(far)
    sibling_wait()

    for mine in (False, True):
        block = mine_qb if mine else 1 - mine_qb
        scores_of(block)
        shares_of(block, mine)

    index_scores()
    seen_bias = packed_bias()
    index_score = ipack[...]
    masked = index_score + seen_bias
    top = both(jnp.max(masked, axis=1, keepdims=True), jnp.maximum)
    tops = jnp.concatenate([top, top], axis=0)
    exp_sum = both(jnp.sum(jnp.exp(masked - tops), axis=1, keepdims=True), jnp.add)
    lse = top + jnp.log(exp_sum)
    for copy in started:
        copy.wait_send()

    def add_share(i, acc):
        exchange(1, lambda to: tsend.at[to], trecv, nh - i, False)
        return acc + trecv[lax.rem(me_h + nh - spread(nh - i), nh)].astype(F32)

    target = lax.fori_loop(1, nh, add_share, town[...]) * (1.0 / HEADS)
    positive = target > 0.0
    logs = jnp.log(jnp.where(positive, target, 1.0))
    gain = both(
        jnp.sum(target * (logs - index_score), axis=1, keepdims=True), jnp.add
    )
    mass = both(jnp.sum(target, axis=1, keepdims=True), jnp.add)
    kl = gain + lse * mass + (1.0 - mass)
    sub = lax.broadcasted_iota(jnp.int32, (8, 128), 0)
    lan = lax.broadcasted_iota(jnp.int32, (8, 128), 1)
    mine = jnp.where(lan == 8 * me_h + sub, kl, 0.0)
    fsend[...] = mine
    lax.fori_loop(1, nh, lambda i, _: exchange(2, lambda to: fsend, frecv, i, True), 0)
    frecv[me_h] = mine
    lax.fori_loop(1, nh, lambda i, _: exchange(2, lambda to: fsend, frecv, i, False), 0)
    out_ref[...] = jnp.sum(jnp.sum(frecv[...], axis=0), axis=0, keepdims=True)


def per_device(
    latent_keys, index_keys, main_query, index_query, index_weight, segment_ids, block_order
):
    rows, kdim = latent_keys.shape
    nc, nh = lax.axis_size("ctx"), lax.axis_size("head")
    ny = nc // 4
    blocks = 2 * nc
    reach = nc // 2 + 1
    heads = main_query.shape[1] // kdim
    iheads = index_weight.shape[1]
    width = (reach - 1) * HALF
    fold = width // 2
    wide = heads * HALF
    half_h = nh // 2
    vmem = pl.BlockSpec(memory_space=pltpu.VMEM)
    hbm = pl.BlockSpec(memory_space=pl.ANY)
    dma = pltpu.SemaphoreType.DMA
    out = pl.pallas_call(
        functools.partial(fused, ny, nh, reach, heads, iheads),
        out_shape=jax.ShapeDtypeStruct((1, rows), F32),
        in_specs=[hbm] * 7,
        out_specs=vmem,
        scratch_shapes=[
            pltpu.VMEM((kdim, rows), BF16),
            pltpu.VMEM((rows, 128), BF16),
            pltpu.VMEM((rows, iheads * 128), BF16),
            pltpu.VMEM((iheads, rows), BF16),
            pltpu.VMEM((blocks * HALF // 128, 128), jnp.int32),
            pltpu.VMEM((1, blocks), jnp.int32),
            pltpu.VMEM((nc, HALF, 2 * kdim + 256), BF16),
            pltpu.VMEM((rows, heads * kdim), BF16),
            pltpu.VMEM((2, wide, LAT + 2 * ROPE), BF16),
            pltpu.VMEM((wide, width), F32),
            pltpu.VMEM((2, HALF, width), F32),
            pltpu.VMEM((8, 16, iheads * 128 + 128), BF16),
            pltpu.VMEM((nh, 16, iheads * 128 + 128), BF16),
            pltpu.VMEM((nh * iheads * 8, 128), BF16),
            pltpu.VMEM((nh * iheads * 8, 128), F32),
            pltpu.VMEM((16, fold), F32),
            pltpu.VMEM((3, 2 * PAD_J, 128), jnp.int32),
            pltpu.SMEM((3, 2 * PAD_J, 128), jnp.int32),
            pltpu.VMEM((nh, 16, fold), BF16),
            pltpu.VMEM((nh, 16, fold), BF16),
            pltpu.VMEM((16, fold), F32),
            pltpu.VMEM((half_h, 16, fold), F32),
            pltpu.VMEM((8, 128), F32),
            pltpu.VMEM((nh, 8, 128), F32),
            dma((2 * (ny - 1) + 6 * ny,)),
            dma((blocks,)),
            dma((3, nh)),
            dma((3, nh)),
            dma((8,)),
            pltpu.SemaphoreType.REGULAR((2,)),
        ],
        compiler_params=pltpu.CompilerParams(
            collective_id=0, has_side_effects=True, vmem_limit_bytes=60 * 2**20
        ),
    )(
        latent_keys.T, index_keys, main_query, index_query, index_weight.T,
        segment_ids.reshape(-1, 128), block_order.reshape(1, blocks),
    )
    return out.reshape(rows)


def solution(mesh):
    in_specs = (
        P("ctx", None),
        P("ctx", None),
        P("ctx", "head"),
        P("ctx", "head"),
        P("ctx", "head"),
        P(),
        P(),
    )
    return jax.shard_map(
        per_device, mesh=mesh, in_specs=in_specs, out_specs=P("ctx"), check_vma=False
    )
```

```python
import functools
import math

import jax
import jax.numpy as jnp
from jax import lax
from jax.experimental import pallas as pl
from jax.experimental.pallas import tpu as pltpu
from jax.sharding import PartitionSpec as P

HEADS = 128
HALF = 64
LAT = 512
ROPE = 64
FILL = -1e30
EXP_SCALE = 192.0 ** (-0.5) * math.log2(math.e)
MESH = pl.DeviceIdType.MESH
NT = (((1,), (1,)), ((), ()))
F32 = jnp.float32
BF16 = jnp.bfloat16
GROUP = 4
UNROLL_M = 4
PAD_J = 24


def dot_nt(a, b):
    return lax.dot_general(a, b, NT, preferred_element_type=F32)


def total_of(x):
    return jnp.sum(jnp.sum(x, axis=1, keepdims=True), axis=0, keepdims=True)


def fused(
    ny, nh, reach, heads, iheads,
    lat_hbm, idx_hbm, mq_hbm, iq_hbm, gain_hbm, seg_hbm, order_hbm,
    out_ref,
    lat_in, idx_in, iq_in, gain_in, seg_in, order_in,
    lat, mraw, mq, score, score_b, bias, iq_send, iq_recv, ilhs, iwide, ipack,
    slot_v, slot_s, tsend, trecv, town, kept, fsend, frecv,
    snd, rcv, xsend, xrecv, local, token,
):
    kdim = LAT + ROPE
    me_c, me_h = lax.axis_index("ctx"), lax.axis_index("head")
    core = me_c % 2
    y = (me_c // 2) % ny
    xl = me_c // (2 * ny)
    xh = me_h % 2
    z = me_h // 2
    nz = nh // 2
    far = ny // 2
    half_h = nh // 2
    width = (reach - 1) * HALF
    fold = width // 2

    def ctx_of(xl_, y_, core_):
        return (xl_ * ny + y_) * 2 + core_

    up = (ctx_of(xl, (y + 1) % ny, core), me_h)
    down = (ctx_of(xl, (y + ny - 1) % ny, core), me_h)
    cross = (
        (ctx_of(1 - xl, y, core), me_h),
        (ctx_of(1 - xl, y, core), z * 2 + 1 - xh),
    )
    sibling = (ctx_of(xl, y, 1 - core), me_h)
    zup = (me_c, ((z + 1) % nz) * 2 + xh)
    zdown = (me_c, ((z + nz - 1) % nz) * 2 + xh)
    twin = (me_c, z * 2 + 1 - xh)
    near = (up, down, cross[0], cross[1], sibling, zup, zdown, twin)

    loads = [
        pltpu.make_async_copy(src, dst, local.at[i])
        for i, (src, dst) in enumerate(
            [
                (lat_hbm, lat_in), (idx_hbm, idx_in), (iq_hbm, iq_in), (gain_hbm, gain_in),
                (seg_hbm, seg_in), (order_hbm, order_in), (mq_hbm, mraw),
            ]
        )
    ]
    for load in loads:
        load.start()
    barrier = pltpu.get_barrier_semaphore()
    for dev in near:
        pl.semaphore_signal(barrier, inc=1, device_id=dev, device_id_type=MESH)

    own = ctx_of(xl, y, core)
    loads[0].wait()
    loads[1].wait()
    keys = jnp.transpose(lat_in[...])
    lat[own, :, 0:LAT] = keys[0:HALF, 0:LAT]
    lat[own, :, LAT:2 * LAT] = keys[HALF:, 0:LAT]
    lat[own, :, 2 * LAT:2 * kdim] = jnp.concatenate([keys[0:HALF, LAT:], keys[HALF:, LAT:]], axis=1)
    for h in (0, 1):
        at = 2 * kdim + h * 128
        lat[own, :, at:at + 128] = idx_in[h * HALF:(h + 1) * HALF, :]

    pl.semaphore_wait(barrier, len(near))

    started = []

    def piece(c, h):
        return lat.at[c, pl.ds(h * (HALF // 2), HALF // 2)], rcv.at[c * 2 + h]

    def send(c, h, dev):
        ref, sem = piece(c, h)
        copy = pltpu.make_async_remote_copy(
            src_ref=ref, dst_ref=ref, send_sem=snd.at[len(started)], recv_sem=sem,
            device_id=dev, device_id_type=MESH,
        )
        copy.start()
        started.append(copy)

    def arrived(c, h):
        ref, sem = piece(c, h)
        pltpu.make_async_remote_copy(
            src_ref=ref, dst_ref=ref, send_sem=snd.at[0], recv_sem=sem,
            device_id=sibling, device_id_type=MESH,
        ).wait_recv()

    def goes(dist, h, way):
        return dist < far or (dist == far and h == way)

    def visits(s):
        for h in (0, 1):
            for way in (0, 1):
                if s == 0 and way == 1:
                    continue
                if s > 0 and not goes(s, h, way):
                    continue
                yield h, way, (y + ny - s) % ny if way == 0 else (y + s) % ny

    def ring_step(s):
        for h, way, yy in visits(s):
            c = ctx_of(xl, yy, core)
            if s > 0:
                arrived(c, h)
            for w in ((0, 1) if s == 0 else (way,)):
                if goes(s + 1, h, w):
                    send(c, h, up if w == 0 else down)
            send(c, h, cross[h])
            send(c, h, sibling)

    def cross_step(s):
        for h, way, yy in visits(s):
            c = ctx_of(1 - xl, yy, core)
            arrived(c, h)
            send(c, h, sibling)

    def sibling_wait():
        for xx in (0, 1):
            for yy in range(ny):
                for h in (0, 1):
                    arrived(ctx_of(xx, yy, 1 - core), h)

    def token_signal():
        pl.semaphore_signal(token.at[0], inc=1, device_id=zup, device_id_type=MESH)
        pl.semaphore_signal(token.at[1], inc=1, device_id=zdown, device_id_type=MESH)

    def token_wait():
        pl.semaphore_wait(token.at[0], 1)
        pl.semaphore_wait(token.at[1], 1)

    def spread(k):
        return half_h + lax.div(k, 2) * (2 * lax.rem(k, 2) - 1)

    def exchange(kind, src, dst, k, start):
        i = spread(k)
        to = lax.rem(me_h + i, nh)
        frm = lax.rem(me_h + nh - i, nh)
        copy = pltpu.make_async_remote_copy(
            src_ref=src(to), dst_ref=dst.at[me_h] if start else dst.at[frm],
            send_sem=xsend.at[kind, to],
            recv_sem=xrecv.at[kind, me_h] if start else xrecv.at[kind, frm],
            device_id=(me_c, to), device_id_type=MESH,
        )
        if start:
            copy.start()
        else:
            copy.wait()
        return 0

    def prepare_small():
        for load in loads[2:6]:
            load.wait()
        gains = jnp.concatenate(
            [gain_in[...].astype(F32), jnp.zeros((128 - iheads, 128), F32)], axis=0
        )
        gains = jnp.transpose(gains).astype(BF16)
        for i in range(8):
            rows = slice(16 * i, 16 * i + 16)
            iq_send[i, :, 0:iheads * 128] = iq_in[rows, :]
            iq_send[i, :, iheads * 128:] = gains[rows, :]
        order = order_in[...]
        blocks = order.shape[1]
        lane = lax.broadcasted_iota(jnp.int32, (1, blocks), 1)
        segs = seg_in[...].astype(F32)
        seg_row = lax.broadcasted_iota(jnp.int32, segs.shape, 0).astype(F32)
        counts = [total_of(jnp.where(segs == float(v), 1.0, 0.0)) for v in range(7)]
        for qb in (0, 1):
            mine_i = jnp.sum(jnp.where(lane == 2 * me_c + qb, order, 0), axis=1, keepdims=True)
            j = lax.broadcasted_iota(jnp.int32, (PAD_J, blocks), 0)
            want = jnp.maximum(mine_i - (reach - 1) + j, 0)
            at = lax.broadcasted_iota(jnp.int32, (PAD_J, blocks), 1)
            slot = jnp.sum(jnp.where(order == want, at, 0), axis=1, keepdims=True)
            slot = jnp.minimum(slot, blocks - 1)
            slot = jnp.broadcast_to(slot, (PAD_J, 128))
            slot_v[0, qb * PAD_J:(qb + 1) * PAD_J, :] = slot
            slot_v[1, qb * PAD_J:(qb + 1) * PAD_J, :] = slot >> 1
            slot_v[2, qb * PAD_J:(qb + 1) * PAD_J, :] = slot & 1
            mine = mine_i.astype(F32)
            first = mine - float(reach - 1)
            pair = jnp.floor(mine * 0.5)
            row = jnp.sum(jnp.where(seg_row == pair, segs, 0.0), axis=0, keepdims=True)
            row = jnp.where(mine - 2.0 * pair > 0.5, pltpu.roll(row, HALF, 1), row)
            sub = lax.broadcasted_iota(jnp.int32, (HALF, 128), 0)
            lan = lax.broadcasted_iota(jnp.int32, (HALF, 128), 1)
            seg_q = jnp.sum(jnp.where(sub == lan, row, 0.0), axis=1, keepdims=True)
            start = jnp.zeros((HALF, 1), F32)
            for v in range(7):
                start = start + jnp.where(seg_q > float(v), counts[v], 0.0)
            pos = mine * float(HALF) + lax.broadcasted_iota(
                jnp.int32, (HALF, 1), 0
            ).astype(F32)
            at = lax.broadcasted_iota(jnp.int32, (HALF, width), 1)
            row_at = lax.broadcasted_iota(jnp.int32, (HALF, width), 0)
            at = at + jnp.where((at < HALF) & (at <= row_at), width, 0)
            kp = first * float(HALF) + at.astype(F32)
            bias[qb] = jnp.where((kp >= start) & (kp <= pos), 0.0, FILL)
        copy = pltpu.make_async_copy(slot_v, slot_s, local.at[7])
        copy.start()
        copy.wait()

    def prepare_queries():
        loads[6].wait()
        for qb in (0, 1):
            for slab in range(4):
                rows = slice(qb * HALF + slab * 16, qb * HALF + slab * 16 + 16)
                for h in range(heads):
                    x = mraw[rows, h * kdim:(h + 1) * kdim]
                    at = slab * 16 * heads + h * 16
                    mq[qb, at:at + 16, 0:LAT] = x[:, 0:LAT]
                    mq[qb, at:at + 16, LAT:] = jnp.concatenate([x[:, LAT:], x[:, LAT:]], axis=1)

    def index_queries():
        def body(i, _):
            exchange(0, lambda to: iq_send.at[to // 2], iq_recv, i, False)
            return 0
        lax.fori_loop(1, nh, body, 0)
        iq_recv[me_h] = iq_send[me_h // 2]
        odd = me_h % 2

        def pick(s, _):
            x = iq_recv[s].astype(F32)
            x = jnp.where(odd == 0, x[0:8], x[8:16])
            at = pl.multiple_of(s * iheads * 8, 16)
            ilhs[pl.ds(at, iheads * 8), :] = jnp.concatenate(
                [x[:, k * 128:(k + 1) * 128] for k in range(iheads)], axis=0
            ).astype(BF16)
            g = x[:, iheads * 128:]
            iwide[pl.ds(at, iheads * 8), :] = jnp.concatenate(
                [jnp.broadcast_to(g[:, k:k + 1], (8, 128)) for k in range(iheads)], axis=0
            )
            return 0

        lax.fori_loop(0, nh, pick, 0)

    mine_qb = me_h // half_h
    mine_row = (me_h % half_h) * 8

    def index_scores():
        rows = ilhs.shape[0]

        def block(j):
            rows = lat[slot_s[1, mine_qb * PAD_J + j, 0]]
            odd = slot_s[2, mine_qb * PAD_J + j, 0]
            lane = lax.broadcasted_iota(jnp.int32, (HALF, 128), 1)
            return jnp.where(
                lane * 0 + odd > 0, rows[:, 2 * kdim + 128:], rows[:, 2 * kdim:2 * kdim + 128]
            )

        def scores(first, count, at):
            ks = [block(first + k) for k in range(count)]
            ks += ks[-1:] * (-count % 2)
            dots = dot_nt(ilhs[...], jnp.concatenate(ks, axis=0))
            for k in range(dots.shape[1] // 128):
                part = jnp.maximum(dots[:, k * 128:(k + 1) * 128], 0.0) * iwide[...]
                part = jnp.sum(part.reshape(rows // 8, 8, 128), axis=0)
                lo = at + k * 128
                if lo < fold:
                    ipack[0:8, lo:lo + 128] = part
                else:
                    ipack[8:16, lo - fold:lo - fold + 128] = part

        for first in range(0, reach - 1, GROUP):
            scores(first, GROUP, first * HALF)
        last = ipack[0:8, 0:128]
        scores(reach - 1, 1, 0)
        lane = lax.broadcasted_iota(jnp.int32, (8, 128), 1)
        row = mine_row + lax.broadcasted_iota(jnp.int32, (8, 128), 0)
        ipack[0:8, 0:128] = jnp.where((lane < HALF) & (lane <= row), ipack[0:8, 0:128], last)

    def packed(x):
        return jnp.concatenate([x[:, 0:fold], x[:, fold:]], axis=0)

    def packed_bias():
        return packed(bias[mine_qb, pl.ds(pl.multiple_of(mine_row, 8), 8), :])

    def both(x, op):
        return op(x[0:8], x[8:16])

    def key_block(qb, j):
        rows = lat[slot_s[1, qb * PAD_J + j, 0]]
        odd = slot_s[2, qb * PAD_J + j, 0]
        lane = lax.broadcasted_iota(jnp.int32, (HALF, 128), 1)
        second = lane * 0 + odd > 0
        second = jnp.concatenate([second] * (LAT // 128), axis=1)
        main = jnp.where(second, rows[:, LAT:2 * LAT], rows[:, 0:LAT])
        tail = rows[:, 2 * LAT:2 * kdim]
        tail = jnp.where(lane // HALF == odd, tail, jnp.zeros_like(tail))
        return jnp.concatenate([main, tail], axis=1)

    def scores_of(qb, score):
        def body(g, _):
            ks = jnp.concatenate([key_block(qb, g * GROUP + k) for k in range(GROUP)], axis=0)
            at = pl.ds(pl.multiple_of(g * GROUP * HALF, 256), GROUP * HALF)
            score[:, at] = dot_nt(mq[qb], ks)
            return 0

        lax.fori_loop(0, (reach - 1) // GROUP, body, 0, unroll=UNROLL_M)
        last = key_block(qb, reach - 1)
        s = dot_nt(mq[qb], jnp.concatenate([last, last], axis=0))
        at = lax.broadcasted_iota(jnp.int32, s.shape, 0)
        row = at // (16 * heads) * 16 + at % 16
        lane = lax.broadcasted_iota(jnp.int32, s.shape, 1)
        score[:, 0:128] = jnp.where((lane < HALF) & (lane <= row), s, score[:, 0:128])

    def shares_of(qb, score):
        def slab(i, _):
            b = bias[qb, pl.ds(pl.multiple_of(i * 16, 16), 16), :]
            acc = jnp.zeros((16, width), F32)
            for h in range(heads):
                at = pl.multiple_of(i * (16 * heads) + h * 16, 16)
                s = score[pl.ds(at, 16), :] + b
                top = jnp.max(s, axis=1, keepdims=True)
                p = jnp.exp2((s - top) * EXP_SCALE)
                acc = acc + p * (1.0 / jnp.sum(p, axis=1, keepdims=True))
            for k in (0, 1):
                share = packed(acc[8 * k:8 * k + 8])
                kept[2 * i + k] = share
                tsend[qb * half_h + 2 * i + k] = share.astype(BF16)
            return 0

        lax.fori_loop(0, 4, slab, 0, unroll=4)

        @pl.when(mine_qb == qb)
        def _():
            town[...] = kept[me_h % half_h]

        def share_send(i, _):
            d = qb * half_h + (me_h + i) % half_h

            @pl.when(d != me_h)
            def _():
                pltpu.make_async_remote_copy(
                    src_ref=tsend.at[d], dst_ref=trecv.at[me_h],
                    send_sem=xsend.at[1, d], recv_sem=xrecv.at[1, me_h],
                    device_id=(me_c, d), device_id_type=MESH,
                ).start()

            return 0

        lax.fori_loop(1, half_h + 1, share_send, 0)

    ring_step(0)
    token_signal()
    prepare_small()
    rounds = nz // 2
    token_wait()
    done = 1
    if done < rounds:
        token_signal()
    prepare_queries()
    for s in range(1, far + 1):
        ring_step(s)
        for _ in range(2):
            if done < rounds:
                token_wait()
                done += 1
                if done < rounds:
                    token_signal()
                else:
                    lax.fori_loop(
                        1, nh,
                        lambda i, _: exchange(0, lambda to: iq_send.at[to // 2], iq_recv, i, True),
                        0,
                    )
        cross_step(s - 1)
    index_queries()
    cross_step(far)
    sibling_wait()

    for qb, table in ((0, score), (1, score_b)):
        scores_of(qb, table)
    for qb, table in ((0, score), (1, score_b)):
        shares_of(qb, table)

    index_scores()
    seen_bias = packed_bias()
    index_score = ipack[...]
    masked = index_score + seen_bias
    top = both(jnp.max(masked, axis=1, keepdims=True), jnp.maximum)
    tops = jnp.concatenate([top, top], axis=0)
    exp_sum = both(jnp.sum(jnp.exp(masked - tops), axis=1, keepdims=True), jnp.add)
    lse = top + jnp.log(exp_sum)
    for copy in started:
        copy.wait_send()

    def add_share(i, acc):
        exchange(1, lambda to: tsend.at[to], trecv, nh - i, False)
        return acc + trecv[lax.rem(me_h + nh - spread(nh - i), nh)].astype(F32)

    target = lax.fori_loop(1, nh, add_share, town[...]) * (1.0 / HEADS)
    positive = target > 0.0
    logs = jnp.log(jnp.where(positive, target, 1.0))
    gain = both(
        jnp.sum(target * (logs - index_score), axis=1, keepdims=True), jnp.add
    )
    mass = both(jnp.sum(target, axis=1, keepdims=True), jnp.add)
    kl = gain + lse * mass + (1.0 - mass)
    sub = lax.broadcasted_iota(jnp.int32, (8, 128), 0)
    lan = lax.broadcasted_iota(jnp.int32, (8, 128), 1)
    mine = jnp.where(lan == 8 * me_h + sub, kl, 0.0)
    fsend[...] = mine
    lax.fori_loop(1, nh, lambda i, _: exchange(2, lambda to: fsend, frecv, i, True), 0)
    frecv[me_h] = mine
    lax.fori_loop(1, nh, lambda i, _: exchange(2, lambda to: fsend, frecv, i, False), 0)
    out_ref[...] = jnp.sum(jnp.sum(frecv[...], axis=0), axis=0, keepdims=True)


def per_device(
    latent_keys, index_keys, main_query, index_query, index_weight, segment_ids, block_order
):
    rows, kdim = latent_keys.shape
    nc, nh = lax.axis_size("ctx"), lax.axis_size("head")
    ny = nc // 4
    blocks = 2 * nc
    reach = nc // 2 + 1
    heads = main_query.shape[1] // kdim
    iheads = index_weight.shape[1]
    width = (reach - 1) * HALF
    fold = width // 2
    wide = heads * HALF
    half_h = nh // 2
    vmem = pl.BlockSpec(memory_space=pltpu.VMEM)
    hbm = pl.BlockSpec(memory_space=pl.ANY)
    dma = pltpu.SemaphoreType.DMA
    out = pl.pallas_call(
        functools.partial(fused, ny, nh, reach, heads, iheads),
        out_shape=jax.ShapeDtypeStruct((1, rows), F32),
        in_specs=[hbm] * 7,
        out_specs=vmem,
        scratch_shapes=[
            pltpu.VMEM((kdim, rows), BF16),
            pltpu.VMEM((rows, 128), BF16),
            pltpu.VMEM((rows, iheads * 128), BF16),
            pltpu.VMEM((iheads, rows), BF16),
            pltpu.VMEM((blocks * HALF // 128, 128), jnp.int32),
            pltpu.VMEM((1, blocks), jnp.int32),
            pltpu.VMEM((nc, HALF, 2 * kdim + 256), BF16),
            pltpu.VMEM((rows, heads * kdim), BF16),
            pltpu.VMEM((2, wide, LAT + 2 * ROPE), BF16),
            pltpu.VMEM((wide, width), F32),
            pltpu.VMEM((wide, width), F32),
            pltpu.VMEM((2, HALF, width), F32),
            pltpu.VMEM((8, 16, iheads * 128 + 128), BF16),
            pltpu.VMEM((nh, 16, iheads * 128 + 128), BF16),
            pltpu.VMEM((nh * iheads * 8, 128), BF16),
            pltpu.VMEM((nh * iheads * 8, 128), F32),
            pltpu.VMEM((16, fold), F32),
            pltpu.VMEM((3, 2 * PAD_J, 128), jnp.int32),
            pltpu.SMEM((3, 2 * PAD_J, 128), jnp.int32),
            pltpu.VMEM((nh, 16, fold), BF16),
            pltpu.VMEM((nh, 16, fold), BF16),
            pltpu.VMEM((16, fold), F32),
            pltpu.VMEM((half_h, 16, fold), F32),
            pltpu.VMEM((8, 128), F32),
            pltpu.VMEM((nh, 8, 128), F32),
            dma((2 * (ny - 1) + 6 * ny,)),
            dma((blocks,)),
            dma((3, nh)),
            dma((3, nh)),
            dma((8,)),
            pltpu.SemaphoreType.REGULAR((2,)),
        ],
        compiler_params=pltpu.CompilerParams(
            collective_id=0, has_side_effects=True, vmem_limit_bytes=60 * 2**20
        ),
    )(
        latent_keys.T, index_keys, main_query, index_query, index_weight.T,
        segment_ids.reshape(-1, 128), block_order.reshape(1, blocks),
    )
    return out.reshape(rows)


def solution(mesh):
    in_specs = (
        P("ctx", None),
        P("ctx", None),
        P("ctx", "head"),
        P("ctx", "head"),
        P("ctx", "head"),
        P(),
        P(),
    )
    return jax.shard_map(
        per_device, mesh=mesh, in_specs=in_specs, out_specs=P("ctx"), check_vma=False
    )
```
